256 devices in a mesh: ep: 128 (over z, x, y), dp: 2 (over core).
Axes of the slice: x: 4, y: 4, z: 8, core: 2. Of those that a mesh axis runs over, the one named last changes fastest.
Arguments:
- tokens: bfloat16 [2, 8192, 2048], P(None, 'ep'), may hold values from -6 to 6
- gate_weights: float32 [2, 8192, 8], P(None, 'ep'), may hold values from 0.1 to 0.5
- expert_ids: int32 [2, 8192, 8], P(None, 'ep'), may hold values from 0 to 127, as said below
- replica: int32 [8192, 8], P('ep'), may hold values from 0 to 839
- spare_plan: int32 [128], replicated, may hold values from 0 to 127, as said below
- w_experts: bfloat16 [128, 2048, 3, 768], P('ep', None, None, 'dp'), may hold values from -0.125 to 0.125
Outputs:
- moe_out: bfloat16 [2, 8192, 2048], P(None, 'ep', 'dp')
The draws below stay inside these ranges and needn't reach their ends.
Inputs may be any that keep to these rules, and one draw needn't show every extreme that they name: `expert_ids`: each token names 8 different experts. `spare_plan`: names an expert for the second slot of every device.
All inputs are finite; a program needn't handle non-finite values.
Results may differ from the reference program's by a relative error of at most 0.0057.
Values may be sent and summed in bfloat16 or wider, within the bound.
No kernel may reach another device: no remote copies, remote signals or barrier semaphores. Data moves between devices by JAX's collectives and lax.ppermute only.
A program may use at most 128 MiB of HBM per device.

```python
import jax
import jax.numpy as jnp
from jax import lax

D = 2048
FF = 768
TOPK = 8
TOK_DEV = 64
CAP1 = 6
CAP2 = 2
EXPERTS = 128
TOKENS = 8192
N_EP = 128


def popularity(key):
    return jax.random.permutation(jax.random.fold_in(key, 11), EXPERTS).astype(jnp.int32)


def draw_expert_ids(key, part):
    standing = popularity(key)
    key = jax.random.fold_in(key, 1)
    noise = jax.random.randint(key, (2, TOKENS, EXPERTS), 0, 4096, dtype=jnp.int32)
    scores = (noise + standing * 2048 // EXPERTS) * EXPERTS + jnp.arange(EXPERTS, dtype=jnp.int32)
    return lax.top_k(scores, TOPK)[1].astype(jnp.int32)


def draw_spare_plan(key, part):
    standing = popularity(key)
    key = jax.random.fold_in(key, 2)
    hottest = jnp.argsort(-standing).astype(jnp.int32)
    owners = jax.random.permutation(key, N_EP)
    assigned = hottest[jnp.arange(N_EP, dtype=jnp.int32) % (N_EP // 4)]
    assigned = assigned.at[0].set(0).at[1].set(EXPERTS - 1)
    return jnp.zeros((N_EP,), jnp.int32).at[owners].set(assigned)


def with_ends(entries, stream_key, low, top_value):
    place = [jax.random.randint(jax.random.fold_in(stream_key, axis), (), 0, length) for axis, length in enumerate(entries.shape)]
    longest = entries.shape.index(max(entries.shape))
    neighbour = place[:longest] + [(place[longest] + 1) % entries.shape[longest]] + place[longest + 1:]
    return entries.at[tuple(place)].set(low).at[tuple(neighbour)].set(top_value)


def shard_levels(rng, shape, cuts, smallest, top_value):
    loudness, own = 1.0, jax.random.fold_in(rng, 6)
    for dim, shards_of in cuts:
        draws = jnp.exp(jax.random.uniform(jax.random.fold_in(own, dim), (shards_of,), jnp.float32, smallest / len(cuts), top_value / len(cuts)))
        loudness = loudness * jnp.repeat(draws, shape[dim] // shards_of).reshape([-1 if axis == dim else 1 for axis in range(len(shape))])
    return loudness


def bell_draw(stream_key, dims, spread, reach, shards=(), kind=jnp.bfloat16):
    result = jax.random.normal(stream_key, dims, jnp.float32) * spread
    if len(shards) > 0:
        result = shard_levels(stream_key, dims, shards, -0.22, 0.18) * result
    return jnp.clip(result, min=-reach, max=reach).astype(kind)


def setup_inputs(seed: int = 0) -> dict:
    splits = jax.random.split(jax.random.key(seed), 7)
    tokens = bell_draw(splits[0], (2, TOKENS, D), 1.0, 6.0, ((1, 128),))
    gate_weights = jnp.clip(0.1 + 0.4 * jax.random.uniform(splits[1], (2, TOKENS, TOPK), jnp.float32) ** shard_levels(splits[1], (2, TOKENS, TOPK), ((1, 128),), -0.2, 0.2), 0.1, 0.5)
    expert_ids = draw_expert_ids(jax.random.fold_in(splits[6], 71), 0)
    replica = with_ends(jax.random.randint(splits[3], (TOKENS, TOPK), 0, 840), jax.random.fold_in(splits[3], 1), 0, 839).astype(jnp.int32)
    spare_plan = draw_spare_plan(jax.random.fold_in(splits[6], 71), 0)
    w_experts = bell_draw(splits[5], (EXPERTS, D, 3, FF), D ** -0.5, 0.125, ((0, 128), (3, 2)))
    return dict(tokens=tokens, gate_weights=gate_weights, expert_ids=expert_ids, replica=replica, spare_plan=spare_plan, w_experts=w_experts)


def hidden_down(token_rows, weights):
    gate_proj = jnp.dot(token_rows, weights[:, 0, :], preferred_element_type=jnp.float32)
    up_proj = jnp.dot(token_rows, weights[:, 1, :], preferred_element_type=jnp.float32)
    hidden = (jax.nn.silu(gate_proj) * up_proj).astype(jnp.bfloat16)
    return lax.dot_general(hidden, weights[:, 2, :], (((1,), (1,)), ((), ())), preferred_element_type=jnp.float32).astype(jnp.bfloat16)


def slot_plan(choices, replicas, spare_plan):
    expert_axis = jnp.arange(EXPERTS, dtype=jnp.int32)
    plan_hot = (spare_plan[:, None] == expert_axis[None, :]).astype(jnp.int32)
    counts = jnp.sum(plan_hot, axis=0)
    spare_rank = jnp.sum((jnp.cumsum(plan_hot, axis=0) - 1) * plan_hot, axis=1)
    replica_pick = replicas % (1 + counts[choices])
    device_axis = jnp.arange(N_EP, dtype=jnp.int32)
    matches = (spare_plan[None, None, :] == choices[:, :, None]) & (spare_rank[None, None, :] == (replica_pick - 1)[:, :, None])
    owner_device = jnp.sum(matches.astype(jnp.int32) * device_axis[None, None, :], axis=2)
    return jnp.where(replica_pick == 0, 2 * choices, 2 * owner_device + 1).astype(jnp.int32)


def run_block(block_tokens, block_gates, slots, slot_count, capacity, expert_of_slot, w_experts):
    rows_dev = TOK_DEV * TOPK
    by_source = slots.reshape(N_EP, rows_dev)
    onehot = (by_source[:, :, None] == jnp.arange(slot_count, dtype=jnp.int32)[None, None, :]).astype(jnp.int32)
    slot_rank = jnp.sum((jnp.cumsum(onehot, axis=1) - 1) * onehot, axis=2)
    kept_rows = slot_rank < capacity
    source = jnp.arange(N_EP, dtype=jnp.int32)[:, None]
    table_size = slot_count * N_EP * capacity
    position = jnp.where(kept_rows, (by_source * N_EP + source) * capacity + slot_rank, table_size)
    row_ids = jnp.arange(N_EP * rows_dev, dtype=jnp.int32)
    slot_table = jnp.full((table_size,), -1, jnp.int32).at[position.reshape(-1)].set(row_ids, mode="drop")
    slot_table = slot_table.reshape(slot_count, N_EP * capacity)
    flat_gates = block_gates.reshape(-1)

    def add_slot(running, inputs):
        table_rows, expert = inputs
        filled = table_rows >= 0
        safe_rows = jnp.maximum(table_rows, 0)
        token_rows = safe_rows // TOPK
        outputs = hidden_down(block_tokens[token_rows], w_experts[expert]).astype(jnp.float32)
        row_scale = jnp.where(filled, flat_gates[safe_rows], jnp.zeros((), jnp.float32))
        return running.at[token_rows].add(outputs * row_scale[:, None]), None

    running = lax.scan(add_slot, jnp.zeros((TOKENS, D), jnp.float32), (slot_table, expert_of_slot))[0]
    return running.astype(jnp.bfloat16)


def reference(tokens, gate_weights, expert_ids, replica, spare_plan, w_experts):
    first_block = run_block(tokens[0], gate_weights[0], expert_ids[0], EXPERTS, CAP1, jnp.arange(EXPERTS, dtype=jnp.int32), w_experts)
    slots = slot_plan(expert_ids[1], replica, spare_plan)
    slot_axis = jnp.arange(2 * N_EP, dtype=jnp.int32)
    expert_of_slot = jnp.where(slot_axis % 2 == 0, slot_axis // 2, spare_plan[slot_axis // 2]).astype(jnp.int32)
    second = run_block(tokens[1], gate_weights[1], slots, 2 * N_EP, CAP2, expert_of_slot, w_experts)
    return jnp.stack([first_block, second], axis=0)
```

```python
import jax
import jax.numpy as jnp
import numpy as np
from jax import lax
from jax.sharding import Mesh
from jax.sharding import PartitionSpec as P

CAP1 = 6
CAP2 = 2
DEPTH = 8
ROW = 4
PLANE = ROW * ROW
BATCH1 = 96
PLANE_AXES = ("x", "y")
ALL_AXES = ("z", "x", "y")
BF16 = jnp.bfloat16
F32 = jnp.float32


def matmul(left, right):
    return jnp.dot(left, right, preferred_element_type=F32)


def kept_gates(gate_weights, expert_ids, replica, spare_plan):
    experts = spare_plan.shape[0]
    tokens = replica.shape[0]
    expert_axis = jnp.arange(experts, dtype=jnp.int32)
    ids = jnp.transpose(expert_ids, (0, 2, 1))[:, :, None, :]
    picked = ids == expert_axis[None, None, :, None]
    gates = jnp.sum(
        jnp.where(picked, jnp.transpose(gate_weights, (0, 2, 1))[:, :, None, :], 0.0), axis=1
    )
    chosen = jnp.any(picked, axis=1)
    replicas = jnp.sum(jnp.where(picked[1], replica.T[:, None, :], 0), axis=0)
    same = spare_plan[:, None] == spare_plan[None, :]
    earlier = expert_axis[None, :] < expert_axis[:, None]
    spare_rank = jnp.sum((same & earlier).astype(jnp.int32), axis=1)
    plan_hot = expert_axis[:, None] == spare_plan[None, :]
    count = jnp.sum(plan_hot.astype(jnp.int32), axis=1)
    pick = jnp.where(chosen[1], lax.rem(replicas, 1 + count[:, None]), -1)
    plan_mat = plan_hot.astype(BF16)
    spare_pick = matmul(plan_mat.T, pick.astype(BF16))
    in_spare = spare_pick == (spare_rank + 1).astype(F32)[:, None]
    members = jnp.concatenate([chosen[0], pick == 0, in_spare], axis=0)
    token_axis = jnp.arange(tokens, dtype=jnp.int32)
    before = (token_axis[:, None] < token_axis[None, :]).astype(BF16)
    ranks = matmul(members.astype(BF16), before)
    limit = jnp.where(jnp.arange(3 * experts) < experts, CAP1, CAP2).astype(F32)
    kept = members & (ranks < limit[:, None])
    spare_kept = matmul(plan_mat, kept[2 * experts :].astype(BF16)) > 0.5
    kept0 = kept[:experts]
    kept1 = kept[experts : 2 * experts] | spare_kept
    table = jnp.concatenate(
        [jnp.where(kept0, gates[0], -1.0), jnp.where(kept1, gates[1], -1.0)], axis=1
    )
    return table, jnp.max(count)


def local(tokens, gate_weights, expert_ids, replica, spare_plan, w_experts):
    half = lax.axis_index("dp")
    count, width = tokens.shape[1], tokens.shape[2]
    share = width // 2
    swap = [(0, 1), (1, 0)]

    mine = lax.dynamic_slice_in_dim(tokens, half * share, share, axis=2)
    gathered = lax.all_gather(mine.reshape(2 * count, share), "z", axis=0)
    gathered = gathered.reshape(DEPTH, 2, count, share)

    table, most = kept_gates(gate_weights, expert_ids, replica, spare_plan)
    table = lax.all_to_all(
        table.reshape(DEPTH, PLANE, 2 * count), "z", split_axis=0, concat_axis=0, tiled=True
    )
    table = jnp.transpose(table.reshape(DEPTH, PLANE, 2, count), (2, 1, 0, 3))
    table = table.reshape(2, PLANE, DEPTH * count)
    kept = table >= 0
    column_axis = jnp.arange(DEPTH * count, dtype=jnp.int32)
    before = (column_axis[:, None] < column_axis[None, :]).astype(BF16)
    places = matmul(kept.reshape(2 * PLANE, -1).astype(BF16), before).reshape(kept.shape)
    places = jnp.where(kept, places, -1.0)
    gates = jnp.maximum(table, 0.0)
    gates_high = gates.astype(BF16)
    gates_low = (gates - gates_high.astype(F32)).astype(BF16)

    home = w_experts[0]
    my_rows = lax.dynamic_slice_in_dim(home, half * share, share, axis=0)
    other_rows = lax.dynamic_slice_in_dim(home, (1 - half) * share, share, axis=0)
    hidden_units = home.shape[2]
    up_mine = my_rows[:, :2, :].reshape(share, 2 * hidden_units)
    up_other = other_rows[:, :2, :].reshape(share, 2 * hidden_units)
    down_mine = my_rows[:, 2, :]
    down_other = lax.ppermute(other_rows[:, 2, :], "dp", swap)

    def contract(left, right):
        return lax.dot_general(left, right, (((1,), (1,)), ((), ())), preferred_element_type=F32)

    def exchange(block, rows, first):
        places_here = places[block]
        slots = (first + jnp.arange(rows, dtype=jnp.int32)).astype(F32)
        hot = places_here[:, None, :] == slots[None, :, None]
        column = gathered[:, block].reshape(DEPTH * count, share)
        picked = matmul(hot.astype(BF16).reshape(PLANE * rows, -1), column).astype(BF16)
        received = lax.all_to_all(
            picked.reshape(PLANE, rows, share), PLANE_AXES, split_axis=0, concat_axis=0, tiled=True
        ).reshape(PLANE * rows, share)
        partner = lax.ppermute(received, "dp", swap)
        both = matmul(received, up_mine) + matmul(partner, up_other)
        hidden = (jax.nn.silu(both[:, :hidden_units]) * both[:, hidden_units:]).astype(BF16)
        partner_hidden = lax.ppermute(hidden, "dp", swap)
        outputs = contract(hidden, down_mine) + contract(partner_hidden, down_other)
        returned = lax.all_to_all(
            outputs.astype(BF16).reshape(PLANE, rows, share),
            PLANE_AXES,
            split_axis=0,
            concat_axis=0,
            tiled=True,
        ).reshape(PLANE * rows, share)

        def combine(part):
            scaled = jnp.where(hot, part[block][:, None, :], 0).astype(BF16)
            return lax.dot_general(
                scaled.reshape(PLANE * rows, -1),
                returned,
                (((0,), (0,)), ((), ())),
                preferred_element_type=F32,
            )

        partial = (combine(gates_high) + combine(gates_low)).astype(BF16)
        return lax.psum_scatter(
            partial.reshape(DEPTH, count, share), "z", scatter_dimension=0, tiled=True
        ).reshape(count, share)

    first = exchange(0, DEPTH * CAP1, 0)
    second = exchange(1, BATCH1, 0).astype(F32)
    most_rows = DEPTH * jnp.minimum(CAP2 * (1 + most), count)
    rounds = (most_rows + BATCH1 - 1) // BATCH1
    second = lax.fori_loop(
        1, rounds, lambda r, total: total + exchange(1, BATCH1, r * BATCH1).astype(F32), second
    ).astype(BF16)
    return jnp.stack([first, second], axis=0)


def solution(mesh):
    grid = Mesh(
        np.asarray(mesh.devices).reshape(DEPTH, ROW, ROW, 2), ("z", "x", "y", "dp")
    )
    in_specs = (
        P(None, ALL_AXES, None),
        P(None, ALL_AXES, None),
        P(None, ALL_AXES, None),
        P(ALL_AXES, None),
        P(),
        P(ALL_AXES, None, None, "dp"),
    )
    out_specs = P(None, ALL_AXES, "dp")
    return jax.shard_map(local, mesh=grid, in_specs=in_specs, out_specs=out_specs, check_vma=False)
```

```python
import jax
import jax.numpy as jnp
import numpy as np
from jax import lax
from jax.experimental import pallas as pl
from jax.experimental.pallas import tpu as pltpu
from jax.sharding import Mesh
from jax.sharding import PartitionSpec as P

CAP1 = 6
CAP2 = 2
DEPTH = 8
ROW = 4
PLANE = ROW * ROW
BATCH0 = DEPTH * CAP1
BATCH1 = 96
TILE = 384
PLANE_AXES = ("x", "y")
ALL_AXES = ("z", "x", "y")
SWAP = [(0, 1), (1, 0)]
BF16 = jnp.bfloat16
F32 = jnp.float32


def matmul(left, right):
    return jnp.dot(left, right, preferred_element_type=F32)


def matmul_nt(left, right):
    return lax.dot_general(left, right, (((1,), (1,)), ((), ())), preferred_element_type=F32)


def matmul_tn(left, right):
    return lax.dot_general(left, right, (((0,), (0,)), ((), ())), preferred_element_type=F32)


def shift(block, step):
    return lax.ppermute(block, "z", [(i, (i + step) % DEPTH) for i in range(DEPTH)])


def up_kernel(half, mine, other, w_mine, w_other, out):
    def project(which):
        return matmul(mine[...], w_mine[which]) + matmul(other[...], w_other[which])

    gate = project(0)
    out[...] = (gate / (1 + jnp.exp(-gate)) * project(1)).astype(BF16)


def down_kernel(half, mine, other, w_mine, w_other, out):
    out[...] = (matmul_nt(mine[...], w_mine[0]) + matmul_nt(other[...], w_other[...])).astype(BF16)


def up_project(half, mine, other, weights):
    rows, share = mine.shape
    units = weights.shape[2]
    row_spec = pl.BlockSpec((TILE, share), lambda i, h: (i, 0))
    return pl.pallas_call(
        up_kernel,
        out_shape=jax.ShapeDtypeStruct((rows, units), BF16),
        grid_spec=pltpu.PrefetchScalarGridSpec(
            num_scalar_prefetch=1,
            grid=(rows // TILE,),
            in_specs=[
                row_spec,
                row_spec,
                pl.BlockSpec((2, share, units), lambda i, h: (0, h[0], 0)),
                pl.BlockSpec((2, share, units), lambda i, h: (0, 1 - h[0], 0)),
            ],
            out_specs=pl.BlockSpec((TILE, units), lambda i, h: (i, 0)),
        ),
        compiler_params=pltpu.CompilerParams(vmem_limit_bytes=32 << 20),
        cost_estimate=pl.CostEstimate(
            flops=8 * rows * share * units,
            bytes_accessed=4 * rows * share + 8 * share * units,
            transcendentals=rows * units,
        ),
        name="up_project",
    )(half, mine, other, weights, weights)


def down_project(half, mine, other, weights, w_other):
    rows, units = mine.shape
    share = w_other.shape[0]
    row_spec = pl.BlockSpec((TILE, units), lambda i, h: (i, 0))
    return pl.pallas_call(
        down_kernel,
        out_shape=jax.ShapeDtypeStruct((rows, share), BF16),
        grid_spec=pltpu.PrefetchScalarGridSpec(
            num_scalar_prefetch=1,
            grid=(rows // TILE,),
            in_specs=[
                row_spec,
                row_spec,
                pl.BlockSpec((1, share, units), lambda i, h: (2, h[0], 0)),
                pl.BlockSpec((share, units), lambda i, h: (0, 0)),
            ],
            out_specs=pl.BlockSpec((TILE, share), lambda i, h: (i, 0)),
        ),
        compiler_params=pltpu.CompilerParams(vmem_limit_bytes=32 << 20),
        cost_estimate=pl.CostEstimate(
            flops=4 * rows * share * units,
            bytes_accessed=4 * rows * units + 4 * share * units + 2 * rows * share,
            transcendentals=0,
        ),
        name="down_project",
    )(half, mine, other, weights, w_other)


def kept_gates(gate_weights, expert_ids, replica, spare_plan):
    experts = spare_plan.shape[0]
    tokens = replica.shape[0]
    expert_axis = jnp.arange(experts, dtype=jnp.int32)
    ids = jnp.transpose(expert_ids, (0, 2, 1))[:, :, None, :]
    picked = ids == expert_axis[None, None, :, None]
    gates = jnp.sum(
        jnp.where(picked, jnp.transpose(gate_weights, (0, 2, 1))[:, :, None, :], 0.0), axis=1
    )
    chosen = jnp.any(picked, axis=1)
    replicas = jnp.sum(jnp.where(picked[1], replica.T[:, None, :], 0), axis=0)
    same = spare_plan[:, None] == spare_plan[None, :]
    earlier = expert_axis[None, :] < expert_axis[:, None]
    spare_rank = jnp.sum((same & earlier).astype(jnp.int32), axis=1)
    plan_hot = expert_axis[:, None] == spare_plan[None, :]
    count = jnp.sum(plan_hot.astype(jnp.int32), axis=1)
    pick = jnp.where(chosen[1], lax.rem(replicas, 1 + count[:, None]), -1)
    plan_mat = plan_hot.astype(BF16)
    spare_pick = matmul(plan_mat.T, pick.astype(BF16))
    in_spare = spare_pick == (spare_rank + 1).astype(F32)[:, None]
    members = jnp.concatenate([chosen[0], pick == 0, in_spare], axis=0)
    token_axis = jnp.arange(tokens, dtype=jnp.int32)
    before = (token_axis[:, None] < token_axis[None, :]).astype(BF16)
    ranks = matmul(members.astype(BF16), before)
    limit = jnp.where(jnp.arange(3 * experts) < experts, CAP1, CAP2).astype(F32)
    kept = members & (ranks < limit[:, None])
    spare_kept = matmul(plan_mat, kept[2 * experts :].astype(BF16)) > 0.5
    kept0 = kept[:experts]
    kept1 = kept[experts : 2 * experts] | spare_kept
    table = jnp.concatenate(
        [jnp.where(kept0, gates[0], -1.0), jnp.where(kept1, gates[1], -1.0)], axis=1
    )
    return table, jnp.max(count)


def gather_column(block):
    middle = block.shape[0] // 2
    back2, front2 = shift(block, 2), shift(block, -2)
    back1, front1 = shift(block, 1), shift(block, -1)
    back3, front3 = shift(back2, 1), shift(front2, -1)
    back4 = shift(back2[:middle], 2)
    front4 = shift(front2[middle:], -2)
    return jnp.concatenate(
        [block, back1, back2, back3, back4, front4, front3, front2, front1], axis=0
    )


def scatter_column(far, near):
    middle = far.shape[1] // 2
    sent = far.astype(BF16)
    add2, add6 = shift(sent[0], -1), shift(sent[2], 1)
    add2_half, add6_half = shift(sent[1, :middle], -2), shift(sent[1, middle:], 2)
    one, seven = shift(near[1].astype(BF16), -1), shift(near[4].astype(BF16), 1)
    zeros = jnp.zeros_like(add2_half)
    to2 = near[2] + add2 + jnp.concatenate([add2_half, zeros], axis=0)
    to6 = near[3] + add6 + jnp.concatenate([zeros, add6_half], axis=0)
    two, six = shift(to2.astype(BF16), -2), shift(to6.astype(BF16), 2)
    return near[0] + one + seven + two + six


def exchange_plane(rows):
    wide = rows.reshape(PLANE, -1, rows.shape[1])
    return lax.all_to_all(
        wide, PLANE_AXES, split_axis=0, concat_axis=0, tiled=True
    ).reshape(rows.shape)


def local(tokens, gate_weights, expert_ids, replica, spare_plan, w_experts):
    half = lax.axis_index("dp").astype(jnp.int32)
    depth_index = lax.axis_index("z")
    count, width = tokens.shape[1], tokens.shape[2]
    share = width // 2
    half_arg = half.reshape(1)
    weights = jnp.transpose(w_experts[0], (1, 0, 2))

    mine = lax.dynamic_slice_in_dim(tokens, half * share, share, axis=2)
    column1 = gather_column(mine[1])

    table, most = kept_gates(gate_weights, expert_ids, replica, spare_plan)
    table = table.reshape(DEPTH, PLANE, 2 * count)
    table = lax.dynamic_slice_in_dim(
        jnp.concatenate([table, table], axis=0), depth_index, DEPTH, axis=0
    )
    pieces = [table[0]] + [shift(table[step], step) for step in range(1, DEPTH)]
    table = jnp.stack(
        [
            jnp.concatenate([piece[:, :count] for piece in pieces], axis=1),
            jnp.concatenate([piece[:, count:] for piece in pieces], axis=1),
        ],
        axis=0,
    )
    kept = table >= 0
    column_axis = jnp.arange(DEPTH * count, dtype=jnp.int32)
    before = (column_axis[:, None] < column_axis[None, :]).astype(BF16)
    places = matmul(kept.reshape(2 * PLANE, -1).astype(BF16), before).reshape(kept.shape)
    places = jnp.where(kept, places, -1.0)
    gates = jnp.maximum(table, 0.0)
    gates_high = gates.astype(BF16)
    gates_low = (gates - gates_high.astype(F32)).astype(BF16)

    down_rows = lax.dynamic_slice_in_dim(weights[2], (1 - half) * share, share, axis=0)
    down_other = lax.ppermute(down_rows, "dp", SWAP)

    def hot_rows(block, rows, first):
        slots = (first + jnp.arange(rows, dtype=jnp.int32)).astype(F32)
        return places[block][:, None, :] == slots[None, :, None]

    def pick(block, column, rows, first):
        hot = hot_rows(block, rows, first).astype(BF16).reshape(PLANE * rows, -1)
        return matmul(hot, column).astype(BF16)

    def experts(received):
        partner = lax.ppermute(received, "dp", SWAP)
        hidden = up_project(half_arg, received, partner, weights)
        partner_hidden = lax.ppermute(hidden, "dp", SWAP)
        return down_project(half_arg, hidden, partner_hidden, weights, down_other)

    def combine(block, returned, rows, first):
        hot = hot_rows(block, rows, first)

        def weighted(lo, hi):
            total = 0
            for part in (gates_high, gates_low):
                scaled = jnp.where(hot, part[block][:, None, :], 0).astype(BF16)
                total = total + matmul_tn(
                    scaled[:, :, lo * count : hi * count].reshape(PLANE * rows, -1), returned
                )
            return total.reshape(hi - lo, count, share)

        far = weighted(3, 6)
        near = jnp.concatenate([weighted(0, 3), weighted(6, DEPTH)], axis=0)
        return scatter_column(far, near)

    picked1 = pick(1, column1, BATCH1, 0)
    mine0, _ = lax.optimization_barrier((mine[0], column1))
    column0 = gather_column(mine0)
    received1 = exchange_plane(picked1)
    picked0 = pick(0, column0, BATCH0, 0)
    received1, picked0 = lax.optimization_barrier((received1, picked0))
    received0 = exchange_plane(picked0)
    outputs1 = experts(received1)
    returned1 = exchange_plane(outputs1)
    outputs0 = experts(received0)
    returned0 = exchange_plane(outputs0)
    second = combine(1, returned1, BATCH1, 0)
    first = combine(0, returned0, BATCH0, 0).astype(BF16)

    def another_round(step, total):
        outgoing = pick(1, column1, BATCH1, step * BATCH1)
        returned = exchange_plane(experts(exchange_plane(outgoing)))
        return total + combine(1, returned, BATCH1, step * BATCH1)

    most_rows = DEPTH * jnp.minimum(CAP2 * (1 + most), count)
    rounds = (most_rows + BATCH1 - 1) // BATCH1
    second = lax.fori_loop(1, rounds, another_round, second).astype(BF16)
    return jnp.stack([first, second], axis=0)


def solution(mesh):
    grid = Mesh(np.asarray(mesh.devices).reshape(DEPTH, ROW, ROW, 2), ("z", "x", "y", "dp"))
    in_specs = (
        P(None, ALL_AXES, None),
        P(None, ALL_AXES, None),
        P(None, ALL_AXES, None),
        P(ALL_AXES, None),
        P(),
        P(ALL_AXES, None, None, "dp"),
    )
    out_specs = P(None, ALL_AXES, "dp")
    return jax.shard_map(local, mesh=grid, in_specs=in_specs, out_specs=out_specs, check_vma=False)
```

```python
import functools

import jax
import jax.numpy as jnp
import numpy as np
from jax import lax
from jax.experimental import pallas as pl
from jax.experimental.pallas import tpu as pltpu
from jax.sharding import Mesh
from jax.sharding import PartitionSpec as P

CAP1 = 6
CAP2 = 2
DEPTH = 8
ROW = 4
PLANE = ROW * ROW
BATCH0 = DEPTH * CAP1
BATCH1 = 96
TILE = 384
PLANE_AXES = ("x", "y")
ALL_AXES = ("z", "x", "y")
SWAP = [(0, 1), (1, 0)]
BF16 = jnp.bfloat16
F32 = jnp.float32


def matmul(left, right):
    return jnp.dot(left, right, preferred_element_type=F32)


def matmul_nt(left, right):
    return lax.dot_general(left, right, (((1,), (1,)), ((), ())), preferred_element_type=F32)


def matmul_tn(left, right):
    return lax.dot_general(left, right, (((0,), (0,)), ((), ())), preferred_element_type=F32)


def shift(block, step):
    return lax.ppermute(block, "z", [(i, (i + step) % DEPTH) for i in range(DEPTH)])


def up_kernel(half, mine, other, w_mine, w_other, out):
    def project(which):
        return matmul(mine[...], w_mine[which]) + matmul(other[...], w_other[which])

    gate = project(0)
    out[...] = (gate / (1 + jnp.exp(-gate)) * project(1)).astype(BF16)


def down_kernel(half, mine, other, w_mine, w_other, out):
    out[...] = (matmul_nt(mine[...], w_mine[0]) + matmul_nt(other[...], w_other[...])).astype(BF16)


def up_project(half, mine, other, weights):
    rows, share = mine.shape
    units = weights.shape[2]
    row_spec = pl.BlockSpec((TILE, share), lambda i, h: (i, 0))
    return pl.pallas_call(
        up_kernel,
        out_shape=jax.ShapeDtypeStruct((rows, units), BF16),
        grid_spec=pltpu.PrefetchScalarGridSpec(
            num_scalar_prefetch=1,
            grid=(rows // TILE,),
            in_specs=[
                row_spec,
                row_spec,
                pl.BlockSpec((2, share, units), lambda i, h: (0, h[0], 0)),
                pl.BlockSpec((2, share, units), lambda i, h: (0, 1 - h[0], 0)),
            ],
            out_specs=pl.BlockSpec((TILE, units), lambda i, h: (i, 0)),
        ),
        compiler_params=pltpu.CompilerParams(vmem_limit_bytes=32 << 20),
        cost_estimate=pl.CostEstimate(
            flops=8 * rows * share * units,
            bytes_accessed=4 * rows * share + 8 * share * units,
            transcendentals=rows * units,
        ),
        name="up_project",
    )(half, mine, other, weights, weights)


def down_project(half, mine, other, weights, w_other):
    rows, units = mine.shape
    share = w_other.shape[0]
    row_spec = pl.BlockSpec((TILE, units), lambda i, h: (i, 0))
    return pl.pallas_call(
        down_kernel,
        out_shape=jax.ShapeDtypeStruct((rows, share), BF16),
        grid_spec=pltpu.PrefetchScalarGridSpec(
            num_scalar_prefetch=1,
            grid=(rows // TILE,),
            in_specs=[
                row_spec,
                row_spec,
                pl.BlockSpec((1, share, units), lambda i, h: (2, h[0], 0)),
                pl.BlockSpec((share, units), lambda i, h: (0, 0)),
            ],
            out_specs=pl.BlockSpec((TILE, share), lambda i, h: (i, 0)),
        ),
        compiler_params=pltpu.CompilerParams(vmem_limit_bytes=32 << 20),
        cost_estimate=pl.CostEstimate(
            flops=4 * rows * share * units,
            bytes_accessed=4 * rows * units + 4 * share * units + 2 * rows * share,
            transcendentals=0,
        ),
        name="down_project",
    )(half, mine, other, weights, w_other)


def combine_kernel(first, returned, places, gates, out, group):
    step = pl.program_id(0)
    rows = returned.shape[0] // group
    tokens = places.shape[1]
    slots = (lax.broadcasted_iota(jnp.int32, (rows, tokens), 0) + first[0]).astype(F32)
    high, low = [], []
    for member in range(group):
        expert = pl.ds(step * group + member, 1)
        gate = jnp.where(places[expert, :] == slots, gates[expert, :], 0.0)
        rounded = gate.astype(BF16)
        high.append(rounded)
        low.append((gate - rounded.astype(F32)).astype(BF16))
    block = returned[...]
    total = matmul_tn(jnp.concatenate(high, axis=0), block)
    total += matmul_tn(jnp.concatenate(low, axis=0), block)

    @pl.when(step == 0)
    def _():
        out[...] = total

    @pl.when(step > 0)
    def _():
        out[...] += total


def combine_rows(returned, places, gates, first, rows):
    tokens = places.shape[1]
    share = returned.shape[1]
    group = 4
    table_spec = pl.BlockSpec((PLANE, tokens), lambda i, f: (0, 0))
    return pl.pallas_call(
        functools.partial(combine_kernel, group=group),
        out_shape=jax.ShapeDtypeStruct((tokens, share), F32),
        grid_spec=pltpu.PrefetchScalarGridSpec(
            num_scalar_prefetch=1,
            grid=(PLANE // group,),
            in_specs=[
                pl.BlockSpec((group * rows, share), lambda i, f: (i, 0)),
                table_spec,
                table_spec,
            ],
            out_specs=pl.BlockSpec((tokens, share), lambda i, f: (0, 0)),
        ),
        compiler_params=pltpu.CompilerParams(vmem_limit_bytes=32 << 20),
        cost_estimate=pl.CostEstimate(
            flops=4 * PLANE * rows * tokens * share,
            bytes_accessed=2 * PLANE * rows * share + 4 * tokens * share,
            transcendentals=0,
        ),
        name="combine_rows",
    )(first, returned, places, gates)


def split_gates(gates):
    high = gates.astype(BF16)
    return high, (gates - high.astype(F32)).astype(BF16)


def pack_choices(gate_weights, expert_ids, replica):
    parts = [expert_ids[0], expert_ids[1], replica // 256, replica % 256]
    parts += [*split_gates(gate_weights[0]), *split_gates(gate_weights[1])]
    packed = jnp.concatenate([part.astype(BF16) for part in parts], axis=1)
    return jnp.pad(packed, ((0, 0), (0, 128 - packed.shape[1])))


def plan_tables(spare_plan, first_expert):
    experts = spare_plan.shape[0]
    expert_axis = jnp.arange(experts, dtype=jnp.int32)
    same = spare_plan[:, None] == spare_plan[None, :]
    earlier = expert_axis[None, :] < expert_axis[:, None]
    spare_rank = jnp.sum((same & earlier).astype(jnp.int32), axis=1)
    most = jnp.max(jnp.sum(same.astype(jnp.int32), axis=1))
    plane_experts = first_expert + jnp.arange(PLANE, dtype=jnp.int32)
    plan_hot = plane_experts[:, None] == spare_plan[None, :]
    count = jnp.sum(plan_hot.astype(jnp.int32), axis=1)
    return count, plan_hot.astype(BF16), spare_rank, most


def place_choices(packed, count, plan_mat, spare_rank, first_expert, source_tokens):
    column_tokens = packed.shape[0]
    top = packed.shape[1] // 16
    numbers = packed.T[: 8 * top].astype(F32).reshape(8, top, 1, column_tokens)
    plane_experts = (first_expert + jnp.arange(PLANE, dtype=jnp.int32)).astype(F32)
    picked = numbers[:2] == plane_experts[None, None, :, None]

    def of_choice(which, values):
        return jnp.sum(jnp.where(picked[which], values, 0.0), axis=0)

    gates = jnp.stack(
        [of_choice(0, numbers[4] + numbers[5]), of_choice(1, numbers[6] + numbers[7])], axis=0
    )
    replicas = of_choice(1, numbers[2] * 256 + numbers[3]).astype(jnp.int32)
    chosen = jnp.any(picked, axis=1)
    pick = jnp.where(chosen[1], lax.rem(replicas, 1 + count[:, None]), -1)
    spare_pick = matmul_tn(plan_mat, pick.astype(BF16))
    in_spare = spare_pick == (spare_rank + 1).astype(F32)[:, None]
    members = jnp.concatenate([chosen[0], pick == 0, in_spare], axis=0).astype(BF16)
    axis = jnp.arange(column_tokens, dtype=jnp.int32)
    before = axis[:, None] < axis[None, :]
    one_source = axis[:, None] // source_tokens == axis[None, :] // source_tokens
    ranks = matmul(members, (before & one_source).astype(BF16))
    limit = jnp.where(jnp.arange(members.shape[0]) < PLANE, CAP1, CAP2).astype(F32)
    kept = jnp.where(ranks < limit[:, None], members, 0)
    kept1 = kept[PLANE : 2 * PLANE] + matmul(plan_mat, kept[2 * PLANE :]).astype(BF16)
    kept = jnp.concatenate([kept[:PLANE], kept1], axis=0)
    places = jnp.where(kept > 0, matmul(kept, before.astype(BF16)), -1.0)
    return places.reshape(2, PLANE, column_tokens), gates


def gather_column(block):
    middle = block.shape[0] // 2
    back2, front2 = shift(block, 2), shift(block, -2)
    back1, front1 = shift(block, 1), shift(block, -1)
    back2, front2, back1, front1 = lax.optimization_barrier((back2, front2, back1, front1))
    back3, front3 = shift(back2, 1), shift(front2, -1)
    back4 = shift(back2[:middle], 2)
    front4 = shift(front2[middle:], -2)
    return jnp.concatenate(
        [block, back1, back2, back3, back4, front4, front3, front2, front1], axis=0
    )


def scatter_column(parts):
    middle = parts.shape[1] // 2
    sent = parts.astype(BF16)
    add2, add6 = shift(sent[3], -1), shift(sent[5], 1)
    add2_half, add6_half = shift(sent[4, :middle], -2), shift(sent[4, middle:], 2)
    one, seven = shift(sent[1], -1), shift(sent[7], 1)
    add2, add6, add2_half, add6_half, one, seven = lax.optimization_barrier(
        (add2, add6, add2_half, add6_half, one, seven)
    )
    zeros = jnp.zeros_like(add2_half)
    to2 = parts[2] + add2 + jnp.concatenate([add2_half, zeros], axis=0)
    to6 = parts[6] + add6 + jnp.concatenate([zeros, add6_half], axis=0)
    two, six = shift(to2.astype(BF16), -2), shift(to6.astype(BF16), 2)
    return parts[0] + one + seven + two + six


def exchange_plane(rows):
    wide = rows.reshape(PLANE, -1, rows.shape[1])
    return lax.all_to_all(
        wide, PLANE_AXES, split_axis=0, concat_axis=0, tiled=True
    ).reshape(rows.shape)


def local(tokens, gate_weights, expert_ids, replica, spare_plan, w_experts):
    half = lax.axis_index("dp").astype(jnp.int32)
    count, width = tokens.shape[1], tokens.shape[2]
    share = width // 2
    half_arg = half.reshape(1)
    weights = jnp.transpose(w_experts[0], (1, 0, 2))

    first_expert = lax.axis_index("z").astype(jnp.int32) * PLANE
    mine = lax.dynamic_slice_in_dim(tokens, half * share, share, axis=2)
    packed = pack_choices(gate_weights, expert_ids, replica)
    gathered = gather_column(jnp.concatenate([mine[1], packed], axis=1))
    column1 = gathered[:, :share]
    count_of, plan_mat, spare_rank, most = plan_tables(spare_plan, first_expert)
    places, gates = place_choices(
        gathered[:, share:], count_of, plan_mat, spare_rank, first_expert, count
    )

    down_rows = lax.dynamic_slice_in_dim(weights[2], (1 - half) * share, share, axis=0)
    down_other = lax.ppermute(down_rows, "dp", SWAP)

    def pick(block, column, rows, first):
        slots = (first + jnp.arange(rows, dtype=jnp.int32)).astype(F32)
        hot = places[block][:, None, :] == slots[None, :, None]
        return matmul(hot.astype(BF16).reshape(PLANE * rows, -1), column).astype(BF16)

    def experts(received):
        partner = lax.ppermute(received, "dp", SWAP)
        hidden = up_project(half_arg, received, partner, weights)
        partner_hidden = lax.ppermute(hidden, "dp", SWAP)
        return down_project(half_arg, hidden, partner_hidden, weights, down_other)

    def combine(block, returned, rows, first):
        first = jnp.asarray(first, jnp.int32).reshape(1)
        sums = combine_rows(returned, places[block], gates[block], first, rows)
        return scatter_column(sums.reshape(DEPTH, count, share))

    picked1 = pick(1, column1, BATCH1, 0)
    mine0, _ = lax.optimization_barrier((mine[0], gathered))
    column0 = gather_column(mine0)
    received1 = exchange_plane(picked1)
    picked0 = pick(0, column0, BATCH0, 0)
    received1, picked0 = lax.optimization_barrier((received1, picked0))
    received0 = exchange_plane(picked0)
    outputs1 = experts(received1)
    outputs1, received0 = lax.optimization_barrier((outputs1, received0))
    returned1 = exchange_plane(outputs1)
    outputs0 = experts(received0)
    returned1, outputs0 = lax.optimization_barrier((returned1, outputs0))
    returned0 = exchange_plane(outputs0)
    second = combine(1, returned1, BATCH1, 0)
    first = combine(0, returned0, BATCH0, 0).astype(BF16)

    def another_round(step, total):
        outgoing = pick(1, column1, BATCH1, step * BATCH1)
        returned = exchange_plane(experts(exchange_plane(outgoing)))
        return total + combine(1, returned, BATCH1, step * BATCH1)

    most_rows = DEPTH * jnp.minimum(CAP2 * (1 + most), count)
    rounds = (most_rows + BATCH1 - 1) // BATCH1
    second = lax.fori_loop(1, rounds, another_round, second).astype(BF16)
    return jnp.stack([first, second], axis=0)


def solution(mesh):
    grid = Mesh(np.asarray(mesh.devices).reshape(DEPTH, ROW, ROW, 2), ("z", "x", "y", "dp"))
    in_specs = (
        P(None, ALL_AXES, None),
        P(None, ALL_AXES, None),
        P(None, ALL_AXES, None),
        P(ALL_AXES, None),
        P(),
        P(ALL_AXES, None, None, "dp"),
    )
    out_specs = P(None, ALL_AXES, "dp")
    return jax.shard_map(local, mesh=grid, in_specs=in_specs, out_specs=out_specs, check_vma=False)
```

```python
import functools

import jax
import jax.numpy as jnp
import numpy as np
from jax import lax
from jax.experimental import pallas as pl
from jax.experimental.pallas import tpu as pltpu
from jax.sharding import Mesh
from jax.sharding import PartitionSpec as P

CAP1 = 6
CAP2 = 2
DEPTH = 8
ROW = 4
PLANE = ROW * ROW
BATCH0 = DEPTH * CAP1
BATCH1 = 96
TILE = 384
PLANE_AXES = ("x", "y")
ALL_AXES = ("z", "x", "y")
SWAP = [(0, 1), (1, 0)]
BF16 = jnp.bfloat16
F32 = jnp.float32


def matmul(left, right):
    return jnp.dot(left, right, preferred_element_type=F32)


def matmul_nt(left, right):
    return lax.dot_general(left, right, (((1,), (1,)), ((), ())), preferred_element_type=F32)


def matmul_tn(left, right):
    return lax.dot_general(left, right, (((0,), (0,)), ((), ())), preferred_element_type=F32)


def shift(block, step):
    return lax.ppermute(block, "z", [(i, (i + step) % DEPTH) for i in range(DEPTH)])


def up_kernel(half, mine, other, w_mine, w_other, out):
    def project(which):
        return matmul(mine[...], w_mine[which]) + matmul(other[...], w_other[which])

    gate = project(0)
    out[...] = (gate / (1 + jnp.exp(-gate)) * project(1)).astype(BF16)


def down_kernel(half, mine, other, w_mine, w_other, out):
    out[...] = (matmul_nt(mine[...], w_mine[0]) + matmul_nt(other[...], w_other[...])).astype(BF16)


def up_project(half, mine, other, weights):
    rows, share = mine.shape
    units = weights.shape[2]
    row_spec = pl.BlockSpec((TILE, share), lambda i, h: (i, 0))
    return pl.pallas_call(
        up_kernel,
        out_shape=jax.ShapeDtypeStruct((rows, units), BF16),
        grid_spec=pltpu.PrefetchScalarGridSpec(
            num_scalar_prefetch=1,
            grid=(rows // TILE,),
            in_specs=[
                row_spec,
                row_spec,
                pl.BlockSpec((2, share, units), lambda i, h: (0, h[0], 0)),
                pl.BlockSpec((2, share, units), lambda i, h: (0, 1 - h[0], 0)),
            ],
            out_specs=pl.BlockSpec((TILE, units), lambda i, h: (i, 0)),
        ),
        compiler_params=pltpu.CompilerParams(vmem_limit_bytes=32 << 20),
        cost_estimate=pl.CostEstimate(
            flops=8 * rows * share * units,
            bytes_accessed=4 * rows * share + 8 * share * units,
            transcendentals=rows * units,
        ),
        name="up_project",
    )(half, mine, other, weights, weights)


def down_project(half, mine, other, weights, w_other):
    rows, units = mine.shape
    share = w_other.shape[0]
    row_spec = pl.BlockSpec((TILE, units), lambda i, h: (i, 0))
    return pl.pallas_call(
        down_kernel,
        out_shape=jax.ShapeDtypeStruct((rows, share), BF16),
        grid_spec=pltpu.PrefetchScalarGridSpec(
            num_scalar_prefetch=1,
            grid=(rows // TILE,),
            in_specs=[
                row_spec,
                row_spec,
                pl.BlockSpec((1, share, units), lambda i, h: (2, h[0], 0)),
                pl.BlockSpec((share, units), lambda i, h: (0, 0)),
            ],
            out_specs=pl.BlockSpec((TILE, share), lambda i, h: (i, 0)),
        ),
        compiler_params=pltpu.CompilerParams(vmem_limit_bytes=32 << 20),
        cost_estimate=pl.CostEstimate(
            flops=4 * rows * share * units,
            bytes_accessed=4 * rows * units + 4 * share * units + 2 * rows * share,
            transcendentals=0,
        ),
        name="down_project",
    )(half, mine, other, weights, w_other)


def pack_kernel(half, tokens, gates, ids, replica, out):
    share = tokens.shape[2]
    top, lanes = replica.shape[0], out.shape[1] - share
    out[:, :share] = tokens[0]
    row = lax.broadcasted_iota(jnp.int32, (top, lanes), 0)
    lane = lax.broadcasted_iota(jnp.int32, (top, lanes), 1)
    numbers = [ids[0], ids[1], replica[...] // 256, replica[...] % 256]
    numbers += [*split_gates(gates[0]), *split_gates(gates[1])]
    total = 0
    for index, part in enumerate(numbers):
        spot = (lane == row + index * top).astype(F32).astype(BF16)
        total += matmul_tn(part.astype(F32).astype(BF16), spot)
    out[:, share:] = total.astype(BF16)


def pack_rows(half, tokens, gate_weights, expert_ids, replica):
    count, share = tokens.shape[1], tokens.shape[2] // 2
    top = replica.shape[1]
    whole = pl.BlockSpec((2, top, count), lambda i, h: (0, 0, 0))
    return pl.pallas_call(
        pack_kernel,
        out_shape=jax.ShapeDtypeStruct((count, share + 128), BF16),
        grid_spec=pltpu.PrefetchScalarGridSpec(
            num_scalar_prefetch=1,
            grid=(1,),
            in_specs=[
                pl.BlockSpec((1, count, share), lambda i, h: (1, 0, h[0])),
                whole,
                whole,
                pl.BlockSpec((top, count), lambda i, h: (0, 0)),
            ],
            out_specs=pl.BlockSpec((count, share + 128), lambda i, h: (0, 0)),
        ),
        name="pack_rows",
    )(
        half,
        tokens,
        jnp.transpose(gate_weights, (0, 2, 1)),
        jnp.transpose(expert_ids, (0, 2, 1)),
        replica.T,
    )


def pick_kernel(first, places, *refs, group):
    blocks, out, column = refs[:-2], refs[-2], refs[-1]
    step = pl.program_id(0)
    share = column.shape[1]

    @pl.when(step == 0)
    def _():
        start = 0
        for block in blocks:
            column[pl.ds(start, block.shape[0]), :] = block[:, :share]
            start += block.shape[0]

    rows = out.shape[0] // group
    tokens = places.shape[1]
    slots = (lax.broadcasted_iota(jnp.int32, (rows, tokens), 0) + first[0]).astype(F32)
    hot = [
        jnp.where(places[pl.ds(step * group + member, 1), :] == slots, 1.0, 0.0).astype(BF16)
        for member in range(group)
    ]
    out[...] = matmul(jnp.concatenate(hot, axis=0), column[...]).astype(BF16)


def pick_rows(places, blocks, first, rows, share):
    tokens = places.shape[1]
    group = 4
    return pl.pallas_call(
        functools.partial(pick_kernel, group=group),
        out_shape=jax.ShapeDtypeStruct((PLANE * rows, share), BF16),
        grid_spec=pltpu.PrefetchScalarGridSpec(
            num_scalar_prefetch=1,
            grid=(PLANE // group,),
            in_specs=[pl.BlockSpec((PLANE, tokens), lambda i, f: (0, 0))]
            + [pl.BlockSpec(block.shape, lambda i, f: (0, 0)) for block in blocks],
            out_specs=pl.BlockSpec((group * rows, share), lambda i, f: (i, 0)),
            scratch_shapes=[pltpu.VMEM((tokens, share), BF16)],
        ),
        compiler_params=pltpu.CompilerParams(vmem_limit_bytes=32 << 20),
        cost_estimate=pl.CostEstimate(
            flops=2 * PLANE * rows * tokens * share,
            bytes_accessed=2 * PLANE * rows * share + 2 * tokens * share,
            transcendentals=0,
        ),
        name="pick_rows",
    )(first, places, *blocks)


def combine_kernel(first, returned, places, gates, out, group):
    step = pl.program_id(0)
    rows = returned.shape[0] // group
    tokens = places.shape[1]
    slots = (lax.broadcasted_iota(jnp.int32, (rows, tokens), 0) + first[0]).astype(F32)
    high, low = [], []
    for member in range(group):
        expert = pl.ds(step * group + member, 1)
        gate = jnp.where(places[expert, :] == slots, gates[expert, :], 0.0)
        rounded = gate.astype(BF16)
        high.append(rounded)
        low.append((gate - rounded.astype(F32)).astype(BF16))
    block = returned[...]
    total = matmul_tn(jnp.concatenate(high, axis=0), block)
    total += matmul_tn(jnp.concatenate(low, axis=0), block)

    @pl.when(step == 0)
    def _():
        out[...] = total

    @pl.when(step > 0)
    def _():
        out[...] += total


def combine_rows(returned, places, gates, first, rows):
    tokens = places.shape[1]
    share = returned.shape[1]
    group = 4
    table_spec = pl.BlockSpec((PLANE, tokens), lambda i, f: (0, 0))
    return pl.pallas_call(
        functools.partial(combine_kernel, group=group),
        out_shape=jax.ShapeDtypeStruct((tokens, share), F32),
        grid_spec=pltpu.PrefetchScalarGridSpec(
            num_scalar_prefetch=1,
            grid=(PLANE // group,),
            in_specs=[
                pl.BlockSpec((group * rows, share), lambda i, f: (i, 0)),
                table_spec,
                table_spec,
            ],
            out_specs=pl.BlockSpec((tokens, share), lambda i, f: (0, 0)),
        ),
        compiler_params=pltpu.CompilerParams(vmem_limit_bytes=32 << 20),
        cost_estimate=pl.CostEstimate(
            flops=4 * PLANE * rows * tokens * share,
            bytes_accessed=2 * PLANE * rows * share + 4 * tokens * share,
            transcendentals=0,
        ),
        name="combine_rows",
    )(first, returned, places, gates)


def split_gates(gates):
    high = gates.astype(BF16)
    return high, (gates - high.astype(F32)).astype(BF16)


def plan_tables(spare_plan, first_expert):
    experts = spare_plan.shape[0]
    expert_axis = jnp.arange(experts, dtype=jnp.int32)
    same = spare_plan[:, None] == spare_plan[None, :]
    earlier = expert_axis[None, :] < expert_axis[:, None]
    spare_rank = jnp.sum((same & earlier).astype(jnp.int32), axis=1)
    most = jnp.max(jnp.sum(same.astype(jnp.int32), axis=1))
    plane_experts = first_expert + jnp.arange(PLANE, dtype=jnp.int32)
    plan_hot = plane_experts[:, None] == spare_plan[None, :]
    count = jnp.sum(plan_hot.astype(jnp.int32), axis=1)
    return count, plan_hot.astype(BF16), spare_rank, most


def place_choices(packed, count, plan_mat, spare_rank, first_expert, source_tokens):
    column_tokens = packed.shape[0]
    top = packed.shape[1] // 16
    numbers = packed.T[: 8 * top].astype(F32).reshape(8, top, 1, column_tokens)
    plane_experts = (first_expert + jnp.arange(PLANE, dtype=jnp.int32)).astype(F32)
    picked = numbers[:2] == plane_experts[None, None, :, None]

    def of_choice(which, values):
        return jnp.sum(jnp.where(picked[which], values, 0.0), axis=0)

    gates = jnp.stack(
        [of_choice(0, numbers[4] + numbers[5]), of_choice(1, numbers[6] + numbers[7])], axis=0
    )
    replicas = of_choice(1, numbers[2] * 256 + numbers[3]).astype(jnp.int32)
    chosen = jnp.any(picked, axis=1)
    pick = jnp.where(chosen[1], lax.rem(replicas, 1 + count[:, None]), -1)
    spare_pick = matmul_tn(plan_mat, pick.astype(BF16))
    in_spare = spare_pick == (spare_rank + 1).astype(F32)[:, None]
    members = jnp.concatenate([chosen[0], pick == 0, in_spare], axis=0).astype(BF16)
    axis = jnp.arange(column_tokens, dtype=jnp.int32)
    before = axis[:, None] < axis[None, :]
    one_source = axis[:, None] // source_tokens == axis[None, :] // source_tokens
    ranks = matmul(members, (before & one_source).astype(BF16))
    limit = jnp.where(jnp.arange(members.shape[0]) < PLANE, CAP1, CAP2).astype(F32)
    kept = jnp.where(ranks < limit[:, None], members, 0)
    kept1 = kept[PLANE : 2 * PLANE] + matmul(plan_mat, kept[2 * PLANE :]).astype(BF16)
    kept = jnp.concatenate([kept[:PLANE], kept1], axis=0)
    places = jnp.where(kept > 0, matmul(kept, before.astype(BF16)), -1.0)
    return places.reshape(2, PLANE, column_tokens), gates


def gather_column(block):
    middle = block.shape[0] // 2
    back2, front2 = shift(block, 2), shift(block, -2)
    back1, front1 = shift(block, 1), shift(block, -1)
    back2, front2, back1, front1 = lax.optimization_barrier((back2, front2, back1, front1))
    back3, front3 = shift(back2, 1), shift(front2, -1)
    back4 = shift(back2[:middle], 2)
    front4 = shift(front2[middle:], -2)
    return [block, back1, back2, back3, back4, front4, front3, front2, front1]


def scatter_column(parts):
    middle = parts.shape[1] // 2
    sent = parts.astype(BF16)
    add2, add6 = shift(sent[3], -1), shift(sent[5], 1)
    add2_half, add6_half = shift(sent[4, :middle], -2), shift(sent[4, middle:], 2)
    one, seven = shift(sent[1], -1), shift(sent[7], 1)
    zeros = jnp.zeros_like(add2_half)
    to2 = parts[2] + add2 + jnp.concatenate([add2_half, zeros], axis=0)
    to6 = parts[6] + add6 + jnp.concatenate([zeros, add6_half], axis=0)
    two, six = shift(to2.astype(BF16), -2), shift(to6.astype(BF16), 2)
    return parts[0] + one + seven + two + six


def exchange_plane(rows):
    wide = rows.reshape(PLANE, -1, rows.shape[1])
    return lax.all_to_all(
        wide, PLANE_AXES, split_axis=0, concat_axis=0, tiled=True
    ).reshape(rows.shape)


def local(tokens, gate_weights, expert_ids, replica, spare_plan, w_experts):
    half = lax.axis_index("dp").astype(jnp.int32)
    count, width = tokens.shape[1], tokens.shape[2]
    share = width // 2
    half_arg = half.reshape(1)
    weights = jnp.transpose(w_experts[0], (1, 0, 2))

    first_expert = lax.axis_index("z").astype(jnp.int32) * PLANE
    blocks1 = gather_column(pack_rows(half_arg, tokens, gate_weights, expert_ids, replica))
    mine0 = lax.dynamic_slice_in_dim(tokens[0], half * share, share, axis=1)
    down_rows = lax.dynamic_slice(
        weights, (2, (1 - half) * share, 0), (1, share, weights.shape[2])
    )
    down_other = lax.ppermute(down_rows[0], "dp", SWAP)
    blocks1, mine0, down_other = lax.optimization_barrier((blocks1, mine0, down_other))
    packed = jnp.concatenate([block[:, share:] for block in blocks1], axis=0)
    count_of, plan_mat, spare_rank, most = plan_tables(spare_plan, first_expert)
    places, gates = place_choices(packed, count_of, plan_mat, spare_rank, first_expert, count)

    def pick(block, blocks, rows, first):
        first = jnp.asarray(first, jnp.int32).reshape(1)
        return pick_rows(places[block], blocks, first, rows, share)

    def experts(received):
        partner = lax.ppermute(received, "dp", SWAP)
        hidden = up_project(half_arg, received, partner, weights)
        partner_hidden = lax.ppermute(hidden, "dp", SWAP)
        return down_project(half_arg, hidden, partner_hidden, weights, down_other)

    def combine(block, returned, rows, first):
        first = jnp.asarray(first, jnp.int32).reshape(1)
        sums = combine_rows(returned, places[block], gates[block], first, rows)
        return scatter_column(sums.reshape(DEPTH, count, share))

    picked1 = pick(1, blocks1, BATCH1, 0)
    blocks0 = gather_column(mine0)
    received1 = exchange_plane(picked1)
    picked0 = pick(0, blocks0, BATCH0, 0)
    received1, picked0 = lax.optimization_barrier((received1, picked0))
    received0 = exchange_plane(picked0)
    outputs1 = experts(received1)
    outputs1, received0 = lax.optimization_barrier((outputs1, received0))
    returned1 = exchange_plane(outputs1)
    outputs0 = experts(received0)
    returned1, outputs0 = lax.optimization_barrier((returned1, outputs0))
    returned0 = exchange_plane(outputs0)
    second = combine(1, returned1, BATCH1, 0)
    first = combine(0, returned0, BATCH0, 0).astype(BF16)

    def another_round(step, total):
        outgoing = pick(1, blocks1, BATCH1, step * BATCH1)
        returned = exchange_plane(experts(exchange_plane(outgoing)))
        return total + combine(1, returned, BATCH1, step * BATCH1)

    most_rows = DEPTH * jnp.minimum(CAP2 * (1 + most), count)
    rounds = (most_rows + BATCH1 - 1) // BATCH1
    second = lax.fori_loop(1, rounds, another_round, second).astype(BF16)
    return jnp.stack([first, second], axis=0)


def solution(mesh):
    grid = Mesh(np.asarray(mesh.devices).reshape(DEPTH, ROW, ROW, 2), ("z", "x", "y", "dp"))
    in_specs = (
        P(None, ALL_AXES, None),
        P(None, ALL_AXES, None),
        P(None, ALL_AXES, None),
        P(ALL_AXES, None),
        P(),
        P(ALL_AXES, None, None, "dp"),
    )
    out_specs = P(None, ALL_AXES, "dp")
    return jax.shard_map(local, mesh=grid, in_specs=in_specs, out_specs=out_specs, check_vma=False)
```

```python
import functools

import jax
import jax.numpy as jnp
import numpy as np
from jax import lax
from jax.experimental import pallas as pl
from jax.experimental.pallas import tpu as pltpu
from jax.sharding import Mesh
from jax.sharding import PartitionSpec as P

CAP1 = 6
CAP2 = 2
DEPTH = 8
ROW = 4
PLANE = ROW * ROW
BATCH0 = DEPTH * CAP1
BATCH1 = 96
TILE = 384
PLANE_AXES = ("x", "y")
ALL_AXES = ("z", "x", "y")
SWAP = [(0, 1), (1, 0)]
BF16 = jnp.bfloat16
F32 = jnp.float32


def matmul(left, right):
    return jnp.dot(left, right, preferred_element_type=F32)


def matmul_nt(left, right):
    return lax.dot_general(left, right, (((1,), (1,)), ((), ())), preferred_element_type=F32)


def matmul_tn(left, right):
    return lax.dot_general(left, right, (((0,), (0,)), ((), ())), preferred_element_type=F32)


def shift(block, step):
    return lax.ppermute(block, "z", [(i, (i + step) % DEPTH) for i in range(DEPTH)])


def up_kernel(half, mine, other, w_mine, w_other, out):
    def project(which):
        return matmul(mine[...], w_mine[which]) + matmul(other[...], w_other[which])

    gate = project(0)
    out[...] = (gate / (1 + jnp.exp(-gate)) * project(1)).astype(BF16)


def down_kernel(half, mine, other, w_mine, w_other, out):
    out[...] = (matmul_nt(mine[...], w_mine[0]) + matmul_nt(other[...], w_other[...])).astype(BF16)


def up_project(half, mine, other, weights):
    rows, share = mine.shape
    units = weights.shape[2]
    row_spec = pl.BlockSpec((TILE, share), lambda i, h: (i, 0))
    return pl.pallas_call(
        up_kernel,
        out_shape=jax.ShapeDtypeStruct((rows, units), BF16),
        grid_spec=pltpu.PrefetchScalarGridSpec(
            num_scalar_prefetch=1,
            grid=(rows // TILE,),
            in_specs=[
                row_spec,
                row_spec,
                pl.BlockSpec((2, share, units), lambda i, h: (0, h[0], 0)),
                pl.BlockSpec((2, share, units), lambda i, h: (0, 1 - h[0], 0)),
            ],
            out_specs=pl.BlockSpec((TILE, units), lambda i, h: (i, 0)),
        ),
        compiler_params=pltpu.CompilerParams(vmem_limit_bytes=32 << 20),
        cost_estimate=pl.CostEstimate(
            flops=8 * rows * share * units,
            bytes_accessed=4 * rows * share + 8 * share * units,
            transcendentals=rows * units,
        ),
        name="up_project",
    )(half, mine, other, weights, weights)


def down_project(half, mine, other, weights, w_other):
    rows, units = mine.shape
    share = w_other.shape[0]
    row_spec = pl.BlockSpec((TILE, units), lambda i, h: (i, 0))
    return pl.pallas_call(
        down_kernel,
        out_shape=jax.ShapeDtypeStruct((rows, share), BF16),
        grid_spec=pltpu.PrefetchScalarGridSpec(
            num_scalar_prefetch=1,
            grid=(rows // TILE,),
            in_specs=[
                row_spec,
                row_spec,
                pl.BlockSpec((1, share, units), lambda i, h: (2, h[0], 0)),
                pl.BlockSpec((share, units), lambda i, h: (0, 0)),
            ],
            out_specs=pl.BlockSpec((TILE, share), lambda i, h: (i, 0)),
        ),
        compiler_params=pltpu.CompilerParams(vmem_limit_bytes=32 << 20),
        cost_estimate=pl.CostEstimate(
            flops=4 * rows * share * units,
            bytes_accessed=4 * rows * units + 4 * share * units + 2 * rows * share,
            transcendentals=0,
        ),
        name="down_project",
    )(half, mine, other, weights, w_other)


def pack_kernel(half, tokens, gates, ids, replica, out):
    share = tokens.shape[2]
    top, lanes = replica.shape[0], out.shape[1] - share
    out[:, :share] = tokens[0]
    row = lax.broadcasted_iota(jnp.int32, (top, lanes), 0)
    lane = lax.broadcasted_iota(jnp.int32, (top, lanes), 1)
    numbers = [ids[0], ids[1], replica[...] // 256, replica[...] % 256]
    numbers += [*split_gates(gates[0]), *split_gates(gates[1])]
    total = 0
    for index, part in enumerate(numbers):
        spot = (lane == row + index * top).astype(F32).astype(BF16)
        total += matmul_tn(part.astype(F32).astype(BF16), spot)
    out[:, share:] = total.astype(BF16)


def pack_rows(half, tokens, gate_weights, expert_ids, replica):
    count, share = tokens.shape[1], tokens.shape[2] // 2
    top = replica.shape[1]
    whole = pl.BlockSpec((2, top, count), lambda i, h: (0, 0, 0))
    return pl.pallas_call(
        pack_kernel,
        out_shape=jax.ShapeDtypeStruct((count, share + 128), BF16),
        grid_spec=pltpu.PrefetchScalarGridSpec(
            num_scalar_prefetch=1,
            grid=(1,),
            in_specs=[
                pl.BlockSpec((1, count, share), lambda i, h: (1, 0, h[0])),
                whole,
                whole,
                pl.BlockSpec((top, count), lambda i, h: (0, 0)),
            ],
            out_specs=pl.BlockSpec((count, share + 128), lambda i, h: (0, 0)),
        ),
        name="pack_rows",
    )(
        half,
        tokens,
        jnp.transpose(gate_weights, (0, 2, 1)),
        jnp.transpose(expert_ids, (0, 2, 1)),
        replica.T,
    )


def pick_kernel(first, places, *refs, group):
    blocks, out, column = refs[:-2], refs[-2], refs[-1]
    step = pl.program_id(0)
    share = column.shape[1]

    @pl.when(step == 0)
    def _():
        start = 0
        for block in blocks:
            column[pl.ds(start, block.shape[0]), :] = block[:, :share]
            start += block.shape[0]

    rows = out.shape[0] // group
    tokens = places.shape[1]
    slots = (lax.broadcasted_iota(jnp.int32, (rows, tokens), 0) + first[0]).astype(F32)
    hot = [
        jnp.where(places[pl.ds(step * group + member, 1), :] == slots, 1.0, 0.0).astype(BF16)
        for member in range(group)
    ]
    out[...] = matmul(jnp.concatenate(hot, axis=0), column[...]).astype(BF16)


def pick_rows(places, blocks, first, rows, share):
    tokens = places.shape[1]
    group = 4
    return pl.pallas_call(
        functools.partial(pick_kernel, group=group),
        out_shape=jax.ShapeDtypeStruct((PLANE * rows, share), BF16),
        grid_spec=pltpu.PrefetchScalarGridSpec(
            num_scalar_prefetch=1,
            grid=(PLANE // group,),
            in_specs=[pl.BlockSpec((PLANE, tokens), lambda i, f: (0, 0))]
            + [pl.BlockSpec(block.shape, lambda i, f: (0, 0)) for block in blocks],
            out_specs=pl.BlockSpec((group * rows, share), lambda i, f: (i, 0)),
            scratch_shapes=[pltpu.VMEM((tokens, share), BF16)],
        ),
        compiler_params=pltpu.CompilerParams(vmem_limit_bytes=32 << 20),
        cost_estimate=pl.CostEstimate(
            flops=2 * PLANE * rows * tokens * share,
            bytes_accessed=2 * PLANE * rows * share + 2 * tokens * share,
            transcendentals=0,
        ),
        name="pick_rows",
    )(first, places, *blocks)


def combine_kernel(first, returned, places, gates, out, rounded_out, group, by_device):
    step = pl.program_id(0)
    rows = returned.shape[0] // group
    tokens = places.shape[1]
    count = tokens // DEPTH
    slots = (lax.broadcasted_iota(jnp.int32, (rows, tokens), 0) + first[0]).astype(F32)
    high, low = [], []
    for member in range(group):
        expert = pl.ds(step * group + member, 1)
        gate = jnp.where(places[expert, :] == slots, gates[expert, :], 0.0)
        rounded = gate.astype(BF16)
        high.append(rounded)
        low.append((gate - rounded.astype(F32)).astype(BF16))
    block = returned[...]
    total = matmul_tn(jnp.concatenate(high, axis=0), block)
    total += matmul_tn(jnp.concatenate(low, axis=0), block)

    @pl.when(step == 0)
    def _():
        out[...] = total

    @pl.when(step > 0)
    def _():
        out[...] += total

    @pl.when(step == pl.num_programs(0) - 1)
    def _():
        for back in range(DEPTH):
            device = lax.rem(first[1] - back + DEPTH, DEPTH) if by_device else back
            spot = pl.ds(device * count, count)
            rounded_out[spot, :] = out[back * count : (back + 1) * count, :].astype(BF16)


def combine_rows(returned, places, gates, first, rows, by_device):
    tokens = places.shape[1]
    share = returned.shape[1]
    group = 4
    table_spec = pl.BlockSpec((PLANE, tokens), lambda i, f: (0, 0))
    return pl.pallas_call(
        functools.partial(combine_kernel, group=group, by_device=by_device),
        out_shape=[
            jax.ShapeDtypeStruct((tokens, share), F32),
            jax.ShapeDtypeStruct((tokens, share), BF16),
        ],
        grid_spec=pltpu.PrefetchScalarGridSpec(
            num_scalar_prefetch=1,
            grid=(PLANE // group,),
            in_specs=[
                pl.BlockSpec((group * rows, share), lambda i, f: (i, 0)),
                table_spec,
                table_spec,
            ],
            out_specs=[pl.BlockSpec((tokens, share), lambda i, f: (0, 0))] * 2,
        ),
        compiler_params=pltpu.CompilerParams(vmem_limit_bytes=32 << 20),
        cost_estimate=pl.CostEstimate(
            flops=4 * PLANE * rows * tokens * share,
            bytes_accessed=2 * PLANE * rows * share + 4 * tokens * share,
            transcendentals=0,
        ),
        name="combine_rows",
    )(first, returned, places, gates)


def split_gates(gates):
    high = gates.astype(BF16)
    return high, (gates - high.astype(F32)).astype(BF16)


def place_kernel(first_expert, plan_row, plan_column, *refs, source_tokens):
    blocks, places, gates = refs[:-2], refs[-2], refs[-1]
    packed = jnp.concatenate([block[...] for block in blocks], axis=0)
    tokens, lanes = packed.shape
    top = lanes // 16
    slots = plan_row.shape[1]
    row = lax.broadcasted_iota(jnp.int32, (lanes // 2, lanes), 0)
    lane = lax.broadcasted_iota(jnp.int32, (lanes // 2, lanes), 1)
    numbers = matmul_nt((row == lane).astype(F32).astype(BF16), packed)

    def number(which, choice):
        return numbers[which * top + choice : which * top + choice + 1, :]

    expert = (lax.broadcasted_iota(jnp.int32, (PLANE, tokens), 0) + first_expert[0]).astype(F32)
    none = jnp.zeros((PLANE, tokens), F32)
    chosen0, chosen1, gates0, gates1, replicas = none, none, none, none, none
    for choice in range(top):
        picked = number(0, choice) == expert
        chosen0 = jnp.where(picked, 1.0, chosen0)
        gates0 = jnp.where(picked, number(4, choice) + number(5, choice), gates0)
        picked = number(1, choice) == expert
        chosen1 = jnp.where(picked, 1.0, chosen1)
        gates1 = jnp.where(picked, number(6, choice) + number(7, choice), gates1)
        replicas = jnp.where(picked, number(2, choice) * 256 + number(3, choice), replicas)
    gates[0] = gates0
    gates[1] = gates1

    holder = lax.broadcasted_iota(jnp.int32, (PLANE, slots), 0) + first_expert[0]
    plan_hot = jnp.where(plan_row[...] == holder, 1.0, 0.0)
    options = 1 + jnp.sum(plan_hot, axis=1, keepdims=True)
    pick = replicas - jnp.floor((replicas + 0.5) / options) * options
    pick = jnp.where(chosen1 > 0, pick, -1.0)
    plan_mat = plan_hot.astype(BF16)
    spare_pick = matmul_tn(plan_mat, pick.astype(BF16))
    slot_row = lax.broadcasted_iota(jnp.int32, (slots, slots), 0)
    slot_lane = lax.broadcasted_iota(jnp.int32, (slots, slots), 1)
    same_before = (plan_row[...] == plan_column[...]) & (slot_lane < slot_row)
    spare_rank = jnp.sum(jnp.where(same_before, 1.0, 0.0), axis=1, keepdims=True)
    in_spare = jnp.where(spare_pick == spare_rank + 1, 1.0, 0.0)
    members = jnp.concatenate([chosen0, jnp.where(pick == 0, 1.0, 0.0), in_spare], axis=0)

    row = lax.broadcasted_iota(jnp.int32, (tokens, tokens), 0)
    lane = lax.broadcasted_iota(jnp.int32, (tokens, tokens), 1)
    before = row < lane
    one_source = row // source_tokens == lane // source_tokens
    ranks = matmul(
        members.astype(BF16), jnp.where(before & one_source, 1.0, 0.0).astype(BF16)
    )
    number_row = lax.broadcasted_iota(jnp.int32, members.shape, 0)
    limit = jnp.where(number_row < PLANE, CAP1, CAP2).astype(F32)
    kept = jnp.where(ranks < limit, members, 0.0)
    kept1 = kept[PLANE : 2 * PLANE] + matmul(plan_mat, kept[2 * PLANE :].astype(BF16))
    kept = jnp.concatenate([kept[:PLANE], kept1], axis=0)
    place = matmul(kept.astype(BF16), jnp.where(before, 1.0, 0.0).astype(BF16))
    place = jnp.where(kept > 0, place, -1.0)
    places[0] = place[:PLANE]
    places[1] = place[PLANE:]


def place_choices(blocks, spare_plan, first_expert, share):
    tokens = sum(block.shape[0] for block in blocks)
    slots = spare_plan.shape[0]
    lanes = blocks[0].shape[1] - share
    shape = (2, PLANE, tokens)
    table_spec = pl.BlockSpec(shape, lambda i, f: (0, 0, 0))
    return pl.pallas_call(
        functools.partial(place_kernel, source_tokens=tokens // DEPTH),
        out_shape=[jax.ShapeDtypeStruct(shape, F32)] * 2,
        grid_spec=pltpu.PrefetchScalarGridSpec(
            num_scalar_prefetch=1,
            grid=(1,),
            in_specs=[
                pl.BlockSpec((1, slots), lambda i, f: (0, 0)),
                pl.BlockSpec((slots, 1), lambda i, f: (0, 0)),
            ]
            + [
                pl.BlockSpec((block.shape[0], lanes), lambda i, f: (0, share // lanes))
                for block in blocks
            ],
            out_specs=[table_spec, table_spec],
        ),
        compiler_params=pltpu.CompilerParams(vmem_limit_bytes=32 << 20),
        name="place_choices",
    )(first_expert.reshape(1), spare_plan[None, :], spare_plan[:, None], *blocks)


def gather_column(block):
    middle = block.shape[0] // 2
    back2, front2 = shift(block, 2), shift(block, -2)
    back1, front1 = shift(block, 1), shift(block, -1)
    back2, front2, back1, front1 = lax.optimization_barrier((back2, front2, back1, front1))
    back3, front3 = shift(back2, 1), shift(front2, -1)
    back4 = shift(back2[:middle], 2)
    front4 = shift(front2[middle:], -2)
    return [block, back1, back2, back3, back4, front4, front3, front2, front1]


def scatter_column(parts, sent):
    middle = parts.shape[1] // 2
    add2, add6 = shift(sent[3], -1), shift(sent[5], 1)
    add2_half, add6_half = shift(sent[4, :middle], -2), shift(sent[4, middle:], 2)
    one, seven = shift(sent[1], -1), shift(sent[7], 1)
    zeros = jnp.zeros_like(add2_half)
    to2 = parts[2] + add2 + jnp.concatenate([add2_half, zeros], axis=0)
    to6 = parts[6] + add6 + jnp.concatenate([zeros, add6_half], axis=0)
    two, six = shift(to2.astype(BF16), -2), shift(to6.astype(BF16), 2)
    return parts[0] + one + seven + two + six


def exchange_plane(rows):
    wide = rows.reshape(PLANE, -1, rows.shape[1])
    return lax.all_to_all(
        wide, PLANE_AXES, split_axis=0, concat_axis=0, tiled=True
    ).reshape(rows.shape)


def local(tokens, gate_weights, expert_ids, replica, spare_plan, w_experts):
    half = lax.axis_index("dp").astype(jnp.int32)
    count, share = tokens.shape[1], tokens.shape[2] // 2
    half_arg = half.reshape(1)
    weights = jnp.transpose(w_experts[0], (1, 0, 2))

    first_expert = lax.axis_index("z").astype(jnp.int32) * PLANE
    blocks1 = gather_column(pack_rows(half_arg, tokens, gate_weights, expert_ids, replica))
    mine0 = lax.dynamic_slice_in_dim(tokens[0], half * share, share, axis=1)
    down_rows = lax.dynamic_slice(
        weights, (2, (1 - half) * share, 0), (1, share, weights.shape[2])
    )
    down_other = lax.ppermute(down_rows[0], "dp", SWAP)
    blocks1, mine0, down_other = lax.optimization_barrier((blocks1, mine0, down_other))
    places, gates = place_choices(blocks1, spare_plan, first_expert, share)

    def pick(block, blocks, rows, first):
        first = jnp.asarray(first, jnp.int32).reshape(1)
        return pick_rows(places[block], blocks, first, rows, share)

    def experts(received):
        partner = lax.ppermute(received, "dp", SWAP)
        hidden = up_project(half_arg, received, partner, weights)
        partner_hidden = lax.ppermute(hidden, "dp", SWAP)
        return down_project(half_arg, hidden, partner_hidden, weights, down_other)

    def combine(block, returned, rows, first, by_device):
        first = jnp.stack([jnp.asarray(first, jnp.int32), lax.axis_index("z").astype(jnp.int32)])
        return [
            sums.reshape(DEPTH, count, share)
            for sums in combine_rows(
                returned, places[block], gates[block], first, rows, by_device
            )
        ]

    def sum_second(returned, first):
        _, sums = combine(1, returned, BATCH1, first, True)
        return lax.psum_scatter(sums, "z", scatter_dimension=0, tiled=True)[0].astype(F32)

    picked1 = pick(1, blocks1, BATCH1, 0)
    blocks0 = gather_column(mine0)
    received1 = exchange_plane(picked1)
    picked0 = pick(0, blocks0, BATCH0, 0)
    received1, picked0 = lax.optimization_barrier((received1, picked0))
    received0 = exchange_plane(picked0)
    outputs1 = experts(received1)
    outputs1, received0 = lax.optimization_barrier((outputs1, received0))
    returned1 = exchange_plane(outputs1)
    outputs0 = experts(received0)
    returned1, outputs0 = lax.optimization_barrier((returned1, outputs0))
    returned0 = exchange_plane(outputs0)
    second = sum_second(returned1, 0)
    first = scatter_column(*combine(0, returned0, BATCH0, 0, False)).astype(BF16)

    def another_round(step, total):
        outgoing = pick(1, blocks1, BATCH1, step * BATCH1)
        returned = exchange_plane(experts(exchange_plane(outgoing)))
        return total + sum_second(returned, step * BATCH1)

    same = spare_plan[:, None] == spare_plan[None, :]
    most = jnp.max(jnp.sum(same.astype(jnp.int32), axis=1))
    most_rows = DEPTH * jnp.minimum(CAP2 * (1 + most), count)
    rounds = (most_rows + BATCH1 - 1) // BATCH1
    second = lax.fori_loop(1, rounds, another_round, second).astype(BF16)
    return jnp.stack([first, second], axis=0)


def solution(mesh):
    grid = Mesh(np.asarray(mesh.devices).reshape(DEPTH, ROW, ROW, 2), ("z", "x", "y", "dp"))
    in_specs = (
        P(None, ALL_AXES, None),
        P(None, ALL_AXES, None),
        P(None, ALL_AXES, None),
        P(ALL_AXES, None),
        P(),
        P(ALL_AXES, None, None, "dp"),
    )
    out_specs = P(None, ALL_AXES, "dp")
    return jax.shard_map(local, mesh=grid, in_specs=in_specs, out_specs=out_specs, check_vma=False)
```

```python
import functools

import jax
import jax.numpy as jnp
import numpy as np
from jax import lax
from jax.experimental import pallas as pl
from jax.experimental.pallas import tpu as pltpu
from jax.sharding import Mesh
from jax.sharding import PartitionSpec as P

CAP1 = 6
CAP2 = 2
DEPTH = 8
ROW = 4
PLANE = ROW * ROW
BATCH0 = DEPTH * CAP1
BATCH1 = 96
TILE = 384
PLANE_AXES = ("x", "y")
ALL_AXES = ("z", "x", "y")
SWAP = [(0, 1), (1, 0)]
BF16 = jnp.bfloat16
F32 = jnp.float32


def matmul(left, right):
    return jnp.dot(left, right, preferred_element_type=F32)


def matmul_nt(left, right):
    return lax.dot_general(left, right, (((1,), (1,)), ((), ())), preferred_element_type=F32)


def matmul_tn(left, right):
    return lax.dot_general(left, right, (((0,), (0,)), ((), ())), preferred_element_type=F32)


def shift(block, step):
    return lax.ppermute(block, "z", [(i, (i + step) % DEPTH) for i in range(DEPTH)])


def up_kernel(half, mine, other, w_mine, w_other, out):
    def project(which):
        return matmul(mine[...], w_mine[which]) + matmul(other[...], w_other[which])

    gate = project(0)
    out[...] = (gate / (1 + jnp.exp(-gate)) * project(1)).astype(BF16)


def down_kernel(half, mine, other, w_mine, w_other, out):
    out[...] = (matmul_nt(mine[...], w_mine[0]) + matmul_nt(other[...], w_other[...])).astype(BF16)


def up_project(half, mine, other, weights):
    rows, share = mine.shape
    units = weights.shape[2]
    row_spec = pl.BlockSpec((TILE, share), lambda i, h: (i, 0))
    return pl.pallas_call(
        up_kernel,
        out_shape=jax.ShapeDtypeStruct((rows, units), BF16),
        grid_spec=pltpu.PrefetchScalarGridSpec(
            num_scalar_prefetch=1,
            grid=(rows // TILE,),
            in_specs=[
                row_spec,
                row_spec,
                pl.BlockSpec((2, share, units), lambda i, h: (0, h[0], 0)),
                pl.BlockSpec((2, share, units), lambda i, h: (0, 1 - h[0], 0)),
            ],
            out_specs=pl.BlockSpec((TILE, units), lambda i, h: (i, 0)),
        ),
        compiler_params=pltpu.CompilerParams(vmem_limit_bytes=32 << 20),
        cost_estimate=pl.CostEstimate(
            flops=8 * rows * share * units,
            bytes_accessed=4 * rows * share + 8 * share * units,
            transcendentals=rows * units,
        ),
        name="up_project",
    )(half, mine, other, weights, weights)


def down_project(half, mine, other, weights, w_other):
    rows, units = mine.shape
    share = w_other.shape[0]
    row_spec = pl.BlockSpec((TILE, units), lambda i, h: (i, 0))
    return pl.pallas_call(
        down_kernel,
        out_shape=jax.ShapeDtypeStruct((rows, share), BF16),
        grid_spec=pltpu.PrefetchScalarGridSpec(
            num_scalar_prefetch=1,
            grid=(rows // TILE,),
            in_specs=[
                row_spec,
                row_spec,
                pl.BlockSpec((1, share, units), lambda i, h: (2, h[0], 0)),
                pl.BlockSpec((share, units), lambda i, h: (0, 0)),
            ],
            out_specs=pl.BlockSpec((TILE, share), lambda i, h: (i, 0)),
        ),
        compiler_params=pltpu.CompilerParams(vmem_limit_bytes=32 << 20),
        cost_estimate=pl.CostEstimate(
            flops=4 * rows * share * units,
            bytes_accessed=4 * rows * units + 4 * share * units + 2 * rows * share,
            transcendentals=0,
        ),
        name="down_project",
    )(half, mine, other, weights, w_other)


def pack_kernel(half, tokens, gates, ids, replica, out):
    share = tokens.shape[2]
    top, lanes = replica.shape[0], out.shape[1] - share
    out[:, :share] = tokens[0]
    row = lax.broadcasted_iota(jnp.int32, (top, lanes), 0)
    lane = lax.broadcasted_iota(jnp.int32, (top, lanes), 1)
    numbers = [ids[0], ids[1], replica[...] // 256, replica[...] % 256]
    numbers += [*split_gates(gates[0]), *split_gates(gates[1])]
    total = 0
    for index, part in enumerate(numbers):
        spot = (lane == row + index * top).astype(F32).astype(BF16)
        total += matmul_tn(part.astype(F32).astype(BF16), spot)
    out[:, share:] = total.astype(BF16)


def pack_rows(half, tokens, gate_weights, expert_ids, replica):
    count, share = tokens.shape[1], tokens.shape[2] // 2
    top = replica.shape[1]
    whole = pl.BlockSpec((2, top, count), lambda i, h: (0, 0, 0))
    return pl.pallas_call(
        pack_kernel,
        out_shape=jax.ShapeDtypeStruct((count, share + 128), BF16),
        grid_spec=pltpu.PrefetchScalarGridSpec(
            num_scalar_prefetch=1,
            grid=(1,),
            in_specs=[
                pl.BlockSpec((1, count, share), lambda i, h: (1, 0, h[0])),
                whole,
                whole,
                pl.BlockSpec((top, count), lambda i, h: (0, 0)),
            ],
            out_specs=pl.BlockSpec((count, share + 128), lambda i, h: (0, 0)),
        ),
        name="pack_rows",
    )(
        half,
        tokens,
        jnp.transpose(gate_weights, (0, 2, 1)),
        jnp.transpose(expert_ids, (0, 2, 1)),
        replica.T,
    )


def pick_kernel(first, places, *refs, group):
    blocks, out, column = refs[:-2], refs[-2], refs[-1]
    step = pl.program_id(0)
    share = column.shape[1]

    @pl.when(step == 0)
    def _():
        start = 0
        for block in blocks:
            column[pl.ds(start, block.shape[0]), :] = block[:, :share]
            start += block.shape[0]

    rows = out.shape[0] // group
    tokens = places.shape[1]
    slots = (lax.broadcasted_iota(jnp.int32, (rows, tokens), 0) + first[0]).astype(F32)
    hot = [
        jnp.where(places[pl.ds(step * group + member, 1), :] == slots, 1.0, 0.0).astype(BF16)
        for member in range(group)
    ]
    out[...] = matmul(jnp.concatenate(hot, axis=0), column[...]).astype(BF16)


def pick_rows(places, blocks, first, rows, share):
    tokens = places.shape[1]
    group = 4
    return pl.pallas_call(
        functools.partial(pick_kernel, group=group),
        out_shape=jax.ShapeDtypeStruct((PLANE * rows, share), BF16),
        grid_spec=pltpu.PrefetchScalarGridSpec(
            num_scalar_prefetch=1,
            grid=(PLANE // group,),
            in_specs=[pl.BlockSpec((PLANE, tokens), lambda i, f: (0, 0))]
            + [pl.BlockSpec(block.shape, lambda i, f: (0, 0)) for block in blocks],
            out_specs=pl.BlockSpec((group * rows, share), lambda i, f: (i, 0)),
            scratch_shapes=[pltpu.VMEM((tokens, share), BF16)],
        ),
        compiler_params=pltpu.CompilerParams(vmem_limit_bytes=32 << 20),
        cost_estimate=pl.CostEstimate(
            flops=2 * PLANE * rows * tokens * share,
            bytes_accessed=2 * PLANE * rows * share + 2 * tokens * share,
            transcendentals=0,
        ),
        name="pick_rows",
    )(first, places, *blocks)


def combine_kernel(first, returned, places, gates, out, rounded_out, group):
    step = pl.program_id(0)
    rows = returned.shape[0] // group
    tokens = places.shape[1]
    slots = (lax.broadcasted_iota(jnp.int32, (rows, tokens), 0) + first[0]).astype(F32)
    high, low = [], []
    for member in range(group):
        expert = pl.ds(step * group + member, 1)
        gate = jnp.where(places[expert, :] == slots, gates[expert, :], 0.0)
        rounded = gate.astype(BF16)
        high.append(rounded)
        low.append((gate - rounded.astype(F32)).astype(BF16))
    block = returned[...]
    total = matmul_tn(jnp.concatenate(high, axis=0), block)
    total += matmul_tn(jnp.concatenate(low, axis=0), block)

    @pl.when(step == 0)
    def _():
        out[...] = total

    @pl.when(step > 0)
    def _():
        out[...] += total

    @pl.when(step == pl.num_programs(0) - 1)
    def _():
        rounded_out[...] = out[...].astype(BF16)


def combine_rows(returned, places, gates, first, rows):
    tokens = places.shape[1]
    share = returned.shape[1]
    group = 4
    table_spec = pl.BlockSpec((PLANE, tokens), lambda i, f: (0, 0))
    return pl.pallas_call(
        functools.partial(combine_kernel, group=group),
        out_shape=[
            jax.ShapeDtypeStruct((tokens, share), F32),
            jax.ShapeDtypeStruct((tokens, share), BF16),
        ],
        grid_spec=pltpu.PrefetchScalarGridSpec(
            num_scalar_prefetch=1,
            grid=(PLANE // group,),
            in_specs=[
                pl.BlockSpec((group * rows, share), lambda i, f: (i, 0)),
                table_spec,
                table_spec,
            ],
            out_specs=[pl.BlockSpec((tokens, share), lambda i, f: (0, 0))] * 2,
        ),
        compiler_params=pltpu.CompilerParams(vmem_limit_bytes=32 << 20),
        cost_estimate=pl.CostEstimate(
            flops=4 * PLANE * rows * tokens * share,
            bytes_accessed=2 * PLANE * rows * share + 4 * tokens * share,
            transcendentals=0,
        ),
        name="combine_rows",
    )(first, returned, places, gates)


def split_gates(gates):
    high = gates.astype(BF16)
    return high, (gates - high.astype(F32)).astype(BF16)


def place_kernel(first_expert, plan_row, plan_column, *refs, source_tokens):
    blocks, places, gates = refs[:-2], refs[-2], refs[-1]
    packed = jnp.concatenate([block[...] for block in blocks], axis=0)
    tokens, lanes = packed.shape
    top = lanes // 16
    slots = plan_row.shape[1]
    row = lax.broadcasted_iota(jnp.int32, (lanes // 2, lanes), 0)
    lane = lax.broadcasted_iota(jnp.int32, (lanes // 2, lanes), 1)
    numbers = matmul_nt((row == lane).astype(F32).astype(BF16), packed)

    def number(which, choice):
        return numbers[which * top + choice : which * top + choice + 1, :]

    expert = (lax.broadcasted_iota(jnp.int32, (PLANE, tokens), 0) + first_expert[0]).astype(F32)
    none = jnp.zeros((PLANE, tokens), F32)
    chosen0, chosen1, gates0, gates1, replicas = none, none, none, none, none
    for choice in range(top):
        picked = number(0, choice) == expert
        chosen0 = jnp.where(picked, 1.0, chosen0)
        gates0 = jnp.where(picked, number(4, choice) + number(5, choice), gates0)
        picked = number(1, choice) == expert
        chosen1 = jnp.where(picked, 1.0, chosen1)
        gates1 = jnp.where(picked, number(6, choice) + number(7, choice), gates1)
        replicas = jnp.where(picked, number(2, choice) * 256 + number(3, choice), replicas)
    gates[0] = gates0
    gates[1] = gates1

    holder = lax.broadcasted_iota(jnp.int32, (PLANE, slots), 0) + first_expert[0]
    plan_hot = jnp.where(plan_row[...] == holder, 1.0, 0.0)
    options = 1 + jnp.sum(plan_hot, axis=1, keepdims=True)
    pick = replicas - jnp.floor((replicas + 0.5) / options) * options
    pick = jnp.where(chosen1 > 0, pick, -1.0)
    plan_mat = plan_hot.astype(BF16)
    spare_pick = matmul_tn(plan_mat, pick.astype(BF16))
    slot_row = lax.broadcasted_iota(jnp.int32, (slots, slots), 0)
    slot_lane = lax.broadcasted_iota(jnp.int32, (slots, slots), 1)
    same_before = (plan_row[...] == plan_column[...]) & (slot_lane < slot_row)
    spare_rank = jnp.sum(jnp.where(same_before, 1.0, 0.0), axis=1, keepdims=True)
    in_spare = jnp.where(spare_pick == spare_rank + 1, 1.0, 0.0)
    members = jnp.concatenate([chosen0, jnp.where(pick == 0, 1.0, 0.0), in_spare], axis=0)

    row = lax.broadcasted_iota(jnp.int32, (tokens, tokens), 0)
    lane = lax.broadcasted_iota(jnp.int32, (tokens, tokens), 1)
    before = row < lane
    one_source = row // source_tokens == lane // source_tokens
    ranks = matmul(
        members.astype(BF16), jnp.where(before & one_source, 1.0, 0.0).astype(BF16)
    )
    number_row = lax.broadcasted_iota(jnp.int32, members.shape, 0)
    limit = jnp.where(number_row < PLANE, CAP1, CAP2).astype(F32)
    kept = jnp.where(ranks < limit, members, 0.0)
    kept1 = kept[PLANE : 2 * PLANE] + matmul(plan_mat, kept[2 * PLANE :].astype(BF16))
    kept = jnp.concatenate([kept[:PLANE], kept1], axis=0)
    place = matmul(kept.astype(BF16), jnp.where(before, 1.0, 0.0).astype(BF16))
    place = jnp.where(kept > 0, place, -1.0)
    places[0] = place[:PLANE]
    places[1] = place[PLANE:]


def place_choices(blocks, spare_plan, first_expert, share):
    tokens = sum(block.shape[0] for block in blocks)
    slots = spare_plan.shape[0]
    lanes = blocks[0].shape[1] - share
    shape = (2, PLANE, tokens)
    table_spec = pl.BlockSpec(shape, lambda i, f: (0, 0, 0))
    return pl.pallas_call(
        functools.partial(place_kernel, source_tokens=tokens // DEPTH),
        out_shape=[jax.ShapeDtypeStruct(shape, F32)] * 2,
        grid_spec=pltpu.PrefetchScalarGridSpec(
            num_scalar_prefetch=1,
            grid=(1,),
            in_specs=[
                pl.BlockSpec((1, slots), lambda i, f: (0, 0)),
                pl.BlockSpec((slots, 1), lambda i, f: (0, 0)),
            ]
            + [
                pl.BlockSpec((block.shape[0], lanes), lambda i, f: (0, share // lanes))
                for block in blocks
            ],
            out_specs=[table_spec, table_spec],
        ),
        compiler_params=pltpu.CompilerParams(vmem_limit_bytes=32 << 20),
        name="place_choices",
    )(first_expert.reshape(1), spare_plan[None, :], spare_plan[:, None], *blocks)


def gather_column(block):
    middle = block.shape[0] // 2
    back2, front2 = shift(block, 2), shift(block, -2)
    back1, front1 = shift(block, 1), shift(block, -1)
    back2, front2, back1, front1 = lax.optimization_barrier((back2, front2, back1, front1))
    back3, front3 = shift(back2, 1), shift(front2, -1)
    back4 = shift(back2[:middle], 2)
    front4 = shift(front2[middle:], -2)
    return [block, back1, back2, back3, back4, front4, front3, front2, front1]


def scatter_far(sent):
    middle = sent.shape[1] // 2
    add2, add6 = shift(sent[3], -1), shift(sent[5], 1)
    add2_half, add6_half = shift(sent[4, :middle], -2), shift(sent[4, middle:], 2)
    return add2, add6, add2_half, add6_half


def relay(sums, far):
    add2, add6, add2_half, add6_half = far
    zeros = jnp.zeros_like(add2_half)
    to2 = sums[2] + add2 + jnp.concatenate([add2_half, zeros], axis=0)
    to6 = sums[6] + add6 + jnp.concatenate([zeros, add6_half], axis=0)
    return to2.astype(BF16), to6.astype(BF16)


def scatter_near(blocks):
    one = shift(jnp.stack([sent[1] for _, sent, _ in blocks]), -1)
    seven = shift(jnp.stack([sent[7] for _, sent, _ in blocks]), 1)
    relayed = [relay(sums, far) for sums, _, far in blocks]
    two = shift(jnp.stack([to2 for to2, _ in relayed]), -2)
    six = shift(jnp.stack([to6 for _, to6 in relayed]), 2)
    return [sums[0] for sums, _, _ in blocks], [one, seven, two, six]


def total_near(mine, received):
    return [
        own + sum(part[index].astype(F32) for part in received) for index, own in enumerate(mine)
    ]


def exchange_plane(rows):
    wide = rows.reshape(PLANE, -1, rows.shape[1])
    return lax.all_to_all(
        wide, PLANE_AXES, split_axis=0, concat_axis=0, tiled=True
    ).reshape(rows.shape)


def local(tokens, gate_weights, expert_ids, replica, spare_plan, w_experts):
    half = lax.axis_index("dp").astype(jnp.int32)
    count, share = tokens.shape[1], tokens.shape[2] // 2
    half_arg = half.reshape(1)
    weights = jnp.transpose(w_experts[0], (1, 0, 2))

    first_expert = lax.axis_index("z").astype(jnp.int32) * PLANE
    blocks1 = gather_column(pack_rows(half_arg, tokens, gate_weights, expert_ids, replica))
    later_half, blocks1[1] = lax.optimization_barrier((half, blocks1[1]))
    mine0 = lax.dynamic_slice_in_dim(tokens[0], half * share, share, axis=1)
    blocks1, mine0 = lax.optimization_barrier((blocks1, mine0))
    down_rows = lax.dynamic_slice(
        weights, (2, (1 - later_half) * share, 0), (1, share, weights.shape[2])
    )
    down_other = lax.ppermute(down_rows[0], "dp", SWAP)
    places, gates = place_choices(blocks1, spare_plan, first_expert, share)

    def pick(block, blocks, rows, first):
        first = jnp.asarray(first, jnp.int32).reshape(1)
        return pick_rows(places[block], blocks, first, rows, share)

    def experts(received, down_other):
        partner = lax.ppermute(received, "dp", SWAP)
        hidden = up_project(half_arg, received, partner, weights)
        partner_hidden = lax.ppermute(hidden, "dp", SWAP)
        return down_project(half_arg, hidden, partner_hidden, weights, down_other)

    def combine(block, returned, rows, first):
        first = jnp.asarray(first, jnp.int32).reshape(1)
        return [
            sums.reshape(DEPTH, count, share)
            for sums in combine_rows(returned, places[block], gates[block], first, rows)
        ]

    picked1 = pick(1, blocks1, BATCH1, 0)
    blocks0 = gather_column(mine0)
    received1 = exchange_plane(picked1)
    picked0 = pick(0, blocks0, BATCH0, 0)
    received1, picked0, down_other = lax.optimization_barrier((received1, picked0, down_other))
    received0 = exchange_plane(picked0)
    outputs1 = experts(received1, down_other)
    outputs1, received0 = lax.optimization_barrier((outputs1, received0))
    returned1 = exchange_plane(outputs1)
    outputs0 = experts(received0, down_other)
    returned1, outputs0 = lax.optimization_barrier((returned1, outputs0))
    returned0 = exchange_plane(outputs0)
    sums1, sent1 = combine(1, returned1, BATCH1, 0)
    returned0, far1 = lax.optimization_barrier((returned0, scatter_far(sent1)))
    sums0, sent0 = combine(0, returned0, BATCH0, 0)
    far0 = scatter_far(sent0)
    mine, received = scatter_near([(sums0, sent0, far0), (sums1, sent1, far1)])

    def another_round(step, total):
        outgoing = pick(1, blocks1, BATCH1, step * BATCH1)
        returned = exchange_plane(experts(exchange_plane(outgoing), down_other))
        sums, sent = combine(1, returned, BATCH1, step * BATCH1)
        return total + total_near(*scatter_near([(sums, sent, scatter_far(sent))]))[0]

    def usual():
        return jnp.stack(total_near(mine, received)).astype(BF16)

    def with_more_rounds():
        first, second = total_near(mine, received)
        second = lax.fori_loop(1, rounds, another_round, second)
        return jnp.stack([first, second]).astype(BF16)

    same = spare_plan[:, None] == spare_plan[None, :]
    most = jnp.max(jnp.sum(same.astype(jnp.int32), axis=1))
    most_rows = DEPTH * jnp.minimum(CAP2 * (1 + most), count)
    rounds = (most_rows + BATCH1 - 1) // BATCH1
    return lax.cond(rounds > 1, with_more_rounds, usual)


def solution(mesh):
    grid = Mesh(np.asarray(mesh.devices).reshape(DEPTH, ROW, ROW, 2), ("z", "x", "y", "dp"))
    in_specs = (
        P(None, ALL_AXES, None),
        P(None, ALL_AXES, None),
        P(None, ALL_AXES, None),
        P(ALL_AXES, None),
        P(),
        P(ALL_AXES, None, None, "dp"),
    )
    out_specs = P(None, ALL_AXES, "dp")
    return jax.shard_map(local, mesh=grid, in_specs=in_specs, out_specs=out_specs, check_vma=False)
```

```python
import functools

import jax
import jax.numpy as jnp
import numpy as np
from jax import lax
from jax.experimental import pallas as pl
from jax.experimental.pallas import tpu as pltpu
from jax.sharding import Mesh
from jax.sharding import PartitionSpec as P

CAP1 = 6
CAP2 = 2
DEPTH = 8
ROW = 4
PLANE = ROW * ROW
BATCH0 = DEPTH * CAP1
BATCH1 = 96
TILE = 384
PLANE_AXES = ("x", "y")
ALL_AXES = ("z", "x", "y")
SWAP = [(0, 1), (1, 0)]
IN_VMEM = pl.BlockSpec(memory_space=pltpu.VMEM)
IN_SMEM = pl.BlockSpec(memory_space=pltpu.SMEM)
BF16 = jnp.bfloat16
F32 = jnp.float32


def matmul(left, right):
    return jnp.dot(left, right, preferred_element_type=F32)


def matmul_nt(left, right):
    return lax.dot_general(left, right, (((1,), (1,)), ((), ())), preferred_element_type=F32)


def matmul_tn(left, right):
    return lax.dot_general(left, right, (((0,), (0,)), ((), ())), preferred_element_type=F32)


def shift(block, step):
    return lax.ppermute(block, "z", [(i, (i + step) % DEPTH) for i in range(DEPTH)])


def up_kernel(half, mine, other, w_mine, w_other, out):
    def project(which):
        return matmul(mine[...], w_mine[which]) + matmul(other[...], w_other[which])

    gate = project(0)
    out[...] = (gate / (1 + jnp.exp(-gate)) * project(1)).astype(BF16)


def down_kernel(half, mine, other, w_mine, w_other, out):
    out[...] = (matmul_nt(mine[...], w_mine[0]) + matmul_nt(other[...], w_other[...])).astype(BF16)


def up_project(half, mine, other, weights):
    rows, share = mine.shape
    units = weights.shape[2]
    row_spec = pl.BlockSpec((TILE, share), lambda i, h: (i, 0))
    return pl.pallas_call(
        up_kernel,
        out_shape=jax.ShapeDtypeStruct((rows, units), BF16),
        grid_spec=pltpu.PrefetchScalarGridSpec(
            num_scalar_prefetch=1,
            grid=(rows // TILE,),
            in_specs=[
                row_spec,
                row_spec,
                pl.BlockSpec((2, share, units), lambda i, h: (0, h[0], 0)),
                pl.BlockSpec((2, share, units), lambda i, h: (0, 1 - h[0], 0)),
            ],
            out_specs=pl.BlockSpec((TILE, units), lambda i, h: (i, 0)),
        ),
        compiler_params=pltpu.CompilerParams(vmem_limit_bytes=32 << 20),
        cost_estimate=pl.CostEstimate(
            flops=8 * rows * share * units,
            bytes_accessed=4 * rows * share + 8 * share * units,
            transcendentals=rows * units,
        ),
        name="up_project",
    )(half, mine, other, weights, weights)


def down_project(half, mine, other, weights, w_other):
    rows, units = mine.shape
    share = w_other.shape[0]
    row_spec = pl.BlockSpec((TILE, units), lambda i, h: (i, 0))
    return pl.pallas_call(
        down_kernel,
        out_shape=jax.ShapeDtypeStruct((rows, share), BF16),
        grid_spec=pltpu.PrefetchScalarGridSpec(
            num_scalar_prefetch=1,
            grid=(rows // TILE,),
            in_specs=[
                row_spec,
                row_spec,
                pl.BlockSpec((1, share, units), lambda i, h: (2, h[0], 0)),
                pl.BlockSpec((share, units), lambda i, h: (0, 0)),
            ],
            out_specs=pl.BlockSpec((TILE, share), lambda i, h: (i, 0)),
        ),
        compiler_params=pltpu.CompilerParams(vmem_limit_bytes=32 << 20),
        cost_estimate=pl.CostEstimate(
            flops=4 * rows * share * units,
            bytes_accessed=4 * rows * units + 4 * share * units + 2 * rows * share,
            transcendentals=0,
        ),
        name="down_project",
    )(half, mine, other, weights, w_other)


def split_gates(gates):
    high = gates.astype(BF16)
    return high, (gates - high.astype(F32)).astype(BF16)


def in_order(blocks):
    block, back13, back2, back4, front4, front2, front13 = blocks
    return [
        block[...],
        back13[0],
        back2[...],
        back13[1],
        back4[...],
        front4[...],
        front13[1],
        front2[...],
        front13[0],
    ]


def pack_kernel(half, tokens, gates, ids, replica, out):
    share = tokens.shape[2]
    top, lanes = replica.shape[0], out.shape[1] - share
    out[:, :share] = tokens[0]
    row = lax.broadcasted_iota(jnp.int32, (top, lanes), 0)
    lane = lax.broadcasted_iota(jnp.int32, (top, lanes), 1)
    numbers = [ids[0], ids[1], replica[...] // 256, replica[...] % 256]
    numbers += [*split_gates(gates[0]), *split_gates(gates[1])]
    total = 0
    for index, part in enumerate(numbers):
        spot = (lane == row + index * top).astype(F32).astype(BF16)
        total += matmul_tn(part.astype(F32).astype(BF16), spot)
    out[:, share:] = total.astype(BF16)


def pack_rows(half, tokens, gate_weights, expert_ids, replica):
    count, share = tokens.shape[1], tokens.shape[2] // 2
    top = replica.shape[1]
    whole = pl.BlockSpec((2, top, count), lambda i, h: (0, 0, 0))
    return pl.pallas_call(
        pack_kernel,
        out_shape=jax.ShapeDtypeStruct((count, share + 128), BF16),
        grid_spec=pltpu.PrefetchScalarGridSpec(
            num_scalar_prefetch=1,
            grid=(1,),
            in_specs=[
                pl.BlockSpec((1, count, share), lambda i, h: (1, 0, h[0])),
                whole,
                whole,
                pl.BlockSpec((top, count), lambda i, h: (0, 0)),
            ],
            out_specs=pl.BlockSpec((count, share + 128), lambda i, h: (0, 0)),
        ),
        name="pack_rows",
    )(
        half,
        tokens,
        jnp.transpose(gate_weights, (0, 2, 1)),
        jnp.transpose(expert_ids, (0, 2, 1)),
        replica.T,
    )


def pick_kernel(first, places, *refs, rows, group):
    blocks, out, column = refs[:-2], refs[-2], refs[-1]
    share = column.shape[1]
    start = 0
    for block in in_order(blocks):
        column[start : start + block.shape[0], :] = block[:, :share]
        start += block.shape[0]
    tokens = places.shape[1]
    slots = (lax.broadcasted_iota(jnp.int32, (rows, tokens), 0) + first[0]).astype(F32)
    for expert in range(0, PLANE, group):
        hot = [
            jnp.where(places[member : member + 1, :] == slots, 1.0, 0.0).astype(BF16)
            for member in range(expert, expert + group)
        ]
        picked = matmul(jnp.concatenate(hot, axis=0), column[...]).astype(BF16)
        out[expert * rows : (expert + group) * rows, :] = picked


def pick_rows(places, blocks, first, rows, share):
    tokens = places.shape[1]
    return pl.pallas_call(
        functools.partial(pick_kernel, rows=rows, group=4),
        out_shape=jax.ShapeDtypeStruct((PLANE * rows, share), BF16),
        in_specs=[IN_SMEM, IN_VMEM] + [IN_VMEM] * len(blocks),
        out_specs=IN_VMEM,
        scratch_shapes=[pltpu.VMEM((tokens, share), BF16)],
        compiler_params=pltpu.CompilerParams(vmem_limit_bytes=32 << 20),
        cost_estimate=pl.CostEstimate(
            flops=2 * PLANE * rows * tokens * share,
            bytes_accessed=2 * PLANE * rows * share + 2 * tokens * share,
            transcendentals=0,
        ),
        name="pick_rows",
    )(first, places, *blocks)


def combine_kernel(
    first, returned, places, gates, near, down, up, half_down, half_up, total, *, rows, group
):
    tokens = places.shape[1]
    count = tokens // DEPTH
    slots = (lax.broadcasted_iota(jnp.int32, (rows, tokens), 0) + first[0]).astype(F32)
    for expert in range(0, PLANE, group):
        high, low = [], []
        for member in range(expert, expert + group):
            here = slice(member, member + 1)
            gate = jnp.where(places[here, :] == slots, gates[here, :], 0.0)
            rounded = gate.astype(BF16)
            high.append(rounded)
            low.append((gate - rounded.astype(F32)).astype(BF16))
        block = returned[expert * rows : (expert + group) * rows, :]
        part = matmul_tn(jnp.concatenate(high, axis=0), block)
        part += matmul_tn(jnp.concatenate(low, axis=0), block)
        if expert == 0:
            total[...] = part
        else:
            total[...] += part

    def sums(back, lo=0, hi=count):
        return total[back * count + lo : back * count + hi, :]

    for index, back in enumerate((0, 2, 6)):
        near[index] = sums(back)
    for index, back in enumerate((1, 3)):
        down[index] = sums(back).astype(BF16)
        up[index] = sums(DEPTH - back).astype(BF16)
    half_down[...] = sums(4, hi=count // 2).astype(BF16)
    half_up[...] = sums(4, lo=count // 2).astype(BF16)


def combine_rows(returned, places, gates, first, rows):
    tokens, share = places.shape[1], returned.shape[1]
    count = tokens // DEPTH
    return pl.pallas_call(
        functools.partial(combine_kernel, rows=rows, group=8),
        out_shape=[
            jax.ShapeDtypeStruct((3, count, share), F32),
            jax.ShapeDtypeStruct((2, count, share), BF16),
            jax.ShapeDtypeStruct((2, count, share), BF16),
            jax.ShapeDtypeStruct((count // 2, share), BF16),
            jax.ShapeDtypeStruct((count // 2, share), BF16),
        ],
        in_specs=[IN_SMEM, IN_VMEM, IN_VMEM, IN_VMEM],
        out_specs=[IN_VMEM] * 5,
        scratch_shapes=[pltpu.VMEM((tokens, share), F32)],
        compiler_params=pltpu.CompilerParams(vmem_limit_bytes=32 << 20),
        cost_estimate=pl.CostEstimate(
            flops=4 * PLANE * rows * tokens * share,
            bytes_accessed=2 * PLANE * rows * share + 4 * tokens * share,
            transcendentals=0,
        ),
        name="combine_rows",
    )(first, returned, places, gates)


def place_kernel(first_expert, plan_row, plan_column, *refs, source_tokens):
    blocks, places, gates = refs[:-2], refs[-2], refs[-1]
    packed = jnp.concatenate(in_order(blocks), axis=0)
    tokens, lanes = packed.shape
    top = lanes // 16
    slots = plan_row.shape[1]
    row = lax.broadcasted_iota(jnp.int32, (lanes // 2, lanes), 0)
    lane = lax.broadcasted_iota(jnp.int32, (lanes // 2, lanes), 1)
    numbers = matmul_nt((row == lane).astype(F32).astype(BF16), packed)

    def number(which, choice):
        return numbers[which * top + choice : which * top + choice + 1, :]

    expert = (lax.broadcasted_iota(jnp.int32, (PLANE, tokens), 0) + first_expert[0]).astype(F32)
    none = jnp.zeros((PLANE, tokens), F32)
    chosen0, chosen1, gates0, gates1, replicas = none, none, none, none, none
    for choice in range(top):
        picked = number(0, choice) == expert
        chosen0 = jnp.where(picked, 1.0, chosen0)
        gates0 = jnp.where(picked, number(4, choice) + number(5, choice), gates0)
        picked = number(1, choice) == expert
        chosen1 = jnp.where(picked, 1.0, chosen1)
        gates1 = jnp.where(picked, number(6, choice) + number(7, choice), gates1)
        replicas = jnp.where(picked, number(2, choice) * 256 + number(3, choice), replicas)
    gates[0] = gates0
    gates[1] = gates1

    holder = lax.broadcasted_iota(jnp.int32, (PLANE, slots), 0) + first_expert[0]
    plan_hot = jnp.where(plan_row[...] == holder, 1.0, 0.0)
    options = 1 + jnp.sum(plan_hot, axis=1, keepdims=True)
    pick = replicas - jnp.floor((replicas + 0.5) / options) * options
    pick = jnp.where(chosen1 > 0, pick, -1.0)
    plan_mat = plan_hot.astype(BF16)
    spare_pick = matmul_tn(plan_mat, pick.astype(BF16))
    slot_row = lax.broadcasted_iota(jnp.int32, (slots, slots), 0)
    slot_lane = lax.broadcasted_iota(jnp.int32, (slots, slots), 1)
    same_before = (plan_row[...] == plan_column[...]) & (slot_lane < slot_row)
    spare_rank = jnp.sum(jnp.where(same_before, 1.0, 0.0), axis=1, keepdims=True)
    in_spare = jnp.where(spare_pick == spare_rank + 1, 1.0, 0.0)
    members = jnp.concatenate([chosen0, jnp.where(pick == 0, 1.0, 0.0), in_spare], axis=0)

    row = lax.broadcasted_iota(jnp.int32, (tokens, tokens), 0)
    lane = lax.broadcasted_iota(jnp.int32, (tokens, tokens), 1)
    before = row < lane
    one_source = row // source_tokens == lane // source_tokens
    ranks = matmul(
        members.astype(BF16), jnp.where(before & one_source, 1.0, 0.0).astype(BF16)
    )
    number_row = lax.broadcasted_iota(jnp.int32, members.shape, 0)
    limit = jnp.where(number_row < PLANE, CAP1, CAP2).astype(F32)
    kept = jnp.where(ranks < limit, members, 0.0)
    kept1 = kept[PLANE : 2 * PLANE] + matmul(plan_mat, kept[2 * PLANE :].astype(BF16))
    kept = jnp.concatenate([kept[:PLANE], kept1], axis=0)
    place = matmul(kept.astype(BF16), jnp.where(before, 1.0, 0.0).astype(BF16))
    place = jnp.where(kept > 0, place, -1.0)
    places[0] = place[:PLANE]
    places[1] = place[PLANE:]


def place_choices(blocks, spare_plan, first_expert, share):
    tokens = DEPTH * blocks[0].shape[0]
    slots = spare_plan.shape[0]
    lanes = blocks[0].shape[1] - share

    def choice_spec(block):
        lead = (0,) * (block.ndim - 1)
        return pl.BlockSpec((*block.shape[:-1], lanes), lambda i, f: (*lead, share // lanes))

    shape = (2, PLANE, tokens)
    table_spec = pl.BlockSpec(shape, lambda i, f: (0, 0, 0))
    return pl.pallas_call(
        functools.partial(place_kernel, source_tokens=tokens // DEPTH),
        out_shape=[jax.ShapeDtypeStruct(shape, F32)] * 2,
        grid_spec=pltpu.PrefetchScalarGridSpec(
            num_scalar_prefetch=1,
            grid=(1,),
            in_specs=[
                pl.BlockSpec((1, slots), lambda i, f: (0, 0)),
                pl.BlockSpec((slots, 1), lambda i, f: (0, 0)),
            ]
            + [choice_spec(block) for block in blocks],
            out_specs=[table_spec, table_spec],
        ),
        compiler_params=pltpu.CompilerParams(vmem_limit_bytes=32 << 20),
        name="place_choices",
    )(first_expert.reshape(1), spare_plan[None, :], spare_plan[:, None], *blocks)


def gather_column(block):
    middle = block.shape[0] // 2
    back2, front2 = shift(block, 2), shift(block, -2)
    back4 = shift(back2[:middle], 2)
    front4 = shift(front2[middle:], -2)
    back13 = shift(jnp.stack([block, back2]), 1)
    front13 = shift(jnp.stack([block, front2]), -1)
    return [block, back13, back2, back4, front4, front2, front13]


def scatter_far(down, up, half_down, half_up):
    return shift(down, -1), shift(up, 1), shift(half_down, -2), shift(half_up, 2)


def scatter_near(blocks):
    to2, to6 = [], []
    for near, (down, up, half_down, half_up) in blocks:
        zeros = jnp.zeros_like(half_down)
        add2 = near[1] + down[1] + jnp.concatenate([half_down, zeros], axis=0)
        add6 = near[2] + up[1] + jnp.concatenate([zeros, half_up], axis=0)
        to2.append(add2.astype(BF16))
        to6.append(add6.astype(BF16))
    return shift(jnp.stack(to2), -2), shift(jnp.stack(to6), 2)


def total_column(blocks, two, six):
    return [
        near[0] + down[0] + up[0] + two[index] + six[index]
        for index, (near, (down, up, _, _)) in enumerate(blocks)
    ]


def exchange_plane(rows):
    wide = rows.reshape(PLANE, -1, rows.shape[1])
    return lax.all_to_all(
        wide, PLANE_AXES, split_axis=0, concat_axis=0, tiled=True
    ).reshape(rows.shape)


def local(tokens, gate_weights, expert_ids, replica, spare_plan, w_experts):
    half = lax.axis_index("dp").astype(jnp.int32)
    count, share = tokens.shape[1], tokens.shape[2] // 2
    half_arg = half.reshape(1)
    weights = jnp.transpose(w_experts[0], (1, 0, 2))

    first_expert = lax.axis_index("z").astype(jnp.int32) * PLANE
    blocks1 = gather_column(pack_rows(half_arg, tokens, gate_weights, expert_ids, replica))
    later_half, blocks1[2] = lax.optimization_barrier((half, blocks1[2]))
    mine0 = lax.dynamic_slice_in_dim(tokens[0], half * share, share, axis=1)
    blocks1, mine0 = lax.optimization_barrier((blocks1, mine0))
    down_rows = lax.dynamic_slice(
        weights, (2, (1 - later_half) * share, 0), (1, share, weights.shape[2])
    )
    down_other = lax.ppermute(down_rows[0], "dp", SWAP)
    places, gates = place_choices(blocks1, spare_plan, first_expert, share)

    def pick(block, blocks, rows, first):
        first = jnp.asarray(first, jnp.int32).reshape(1)
        return pick_rows(places[block], blocks, first, rows, share)

    def experts(received, down_other):
        partner = lax.ppermute(received, "dp", SWAP)
        hidden = up_project(half_arg, received, partner, weights)
        partner_hidden = lax.ppermute(hidden, "dp", SWAP)
        return down_project(half_arg, hidden, partner_hidden, weights, down_other)

    def combine(block, returned, rows, first):
        first = jnp.asarray(first, jnp.int32).reshape(1)
        near, *parts = combine_rows(returned, places[block], gates[block], first, rows)
        return near, scatter_far(*parts)

    picked1 = pick(1, blocks1, BATCH1, 0)
    blocks0 = gather_column(mine0)
    received1 = exchange_plane(picked1)
    picked0 = pick(0, blocks0, BATCH0, 0)
    received1, picked0, down_other = lax.optimization_barrier((received1, picked0, down_other))
    received0 = exchange_plane(picked0)
    outputs1 = experts(received1, down_other)
    outputs1, received0 = lax.optimization_barrier((outputs1, received0))
    returned1 = exchange_plane(outputs1)
    outputs0 = experts(received0, down_other)
    returned1, outputs0 = lax.optimization_barrier((returned1, outputs0))
    returned0 = exchange_plane(outputs0)
    second = combine(1, returned1, BATCH1, 0)
    returned0, second = lax.optimization_barrier((returned0, second))
    first = combine(0, returned0, BATCH0, 0)
    two, six = scatter_near([first, second])

    def another_round(step, total):
        outgoing = pick(1, blocks1, BATCH1, step * BATCH1)
        returned = exchange_plane(experts(exchange_plane(outgoing), down_other))
        sums = [combine(1, returned, BATCH1, step * BATCH1)]
        return total + total_column(sums, *scatter_near(sums))[0]

    def usual():
        return jnp.stack(total_column([first, second], two, six)).astype(BF16)

    def with_more_rounds():
        total0, total1 = total_column([first, second], two, six)
        total1 = lax.fori_loop(1, rounds, another_round, total1)
        return jnp.stack([total0, total1]).astype(BF16)

    same = spare_plan[:, None] == spare_plan[None, :]
    most = jnp.max(jnp.sum(same.astype(jnp.int32), axis=1))
    most_rows = DEPTH * jnp.minimum(CAP2 * (1 + most), count)
    rounds = (most_rows + BATCH1 - 1) // BATCH1
    return lax.cond(rounds > 1, with_more_rounds, usual)


def solution(mesh):
    grid = Mesh(np.asarray(mesh.devices).reshape(DEPTH, ROW, ROW, 2), ("z", "x", "y", "dp"))
    in_specs = (
        P(None, ALL_AXES, None),
        P(None, ALL_AXES, None),
        P(None, ALL_AXES, None),
        P(ALL_AXES, None),
        P(),
        P(ALL_AXES, None, None, "dp"),
    )
    out_specs = P(None, ALL_AXES, "dp")
    return jax.shard_map(local, mesh=grid, in_specs=in_specs, out_specs=out_specs, check_vma=False)
```

```python
import functools

import jax
import jax.numpy as jnp
import numpy as np
from jax import lax
from jax.experimental import pallas as pl
from jax.experimental.pallas import tpu as pltpu
from jax.sharding import Mesh
from jax.sharding import PartitionSpec as P

CAP1 = 6
CAP2 = 2
DEPTH = 8
ROW = 4
PLANE = ROW * ROW
BATCH0 = DEPTH * CAP1
BATCH1 = (80, 96)
PLANE_AXES = ("x", "y")
ALL_AXES = ("z", "x", "y")
SWAP = [(0, 1), (1, 0)]
IN_VMEM = pl.BlockSpec(memory_space=pltpu.VMEM)
IN_SMEM = pl.BlockSpec(memory_space=pltpu.SMEM)
BF16 = jnp.bfloat16
F32 = jnp.float32


def matmul(left, right):
    return jnp.dot(left, right, preferred_element_type=F32)


def matmul_nt(left, right):
    return lax.dot_general(left, right, (((1,), (1,)), ((), ())), preferred_element_type=F32)


def matmul_tn(left, right):
    return lax.dot_general(left, right, (((0,), (0,)), ((), ())), preferred_element_type=F32)


def shift(block, step):
    return lax.ppermute(block, "z", [(i, (i + step) % DEPTH) for i in range(DEPTH)])


def tile_of(rows):
    return 384 if rows % 384 == 0 else 320


def up_kernel(half, mine, other, w_mine, w_other, out):
    def project(which):
        return matmul(mine[...], w_mine[which]) + matmul(other[...], w_other[which])

    gate = project(0)
    out[...] = (gate / (1 + jnp.exp(-gate)) * project(1)).astype(BF16)


def down_kernel(half, mine, other, w_mine, w_other, out):
    out[...] = (matmul_nt(mine[...], w_mine[0]) + matmul_nt(other[...], w_other[...])).astype(BF16)


def up_project(half, mine, other, weights):
    rows, share = mine.shape
    units = weights.shape[2]
    tile = tile_of(rows)
    row_spec = pl.BlockSpec((tile, share), lambda i, h: (i, 0))
    return pl.pallas_call(
        up_kernel,
        out_shape=jax.ShapeDtypeStruct((rows, units), BF16),
        grid_spec=pltpu.PrefetchScalarGridSpec(
            num_scalar_prefetch=1,
            grid=(rows // tile,),
            in_specs=[
                row_spec,
                row_spec,
                pl.BlockSpec((2, share, units), lambda i, h: (0, h[0], 0)),
                pl.BlockSpec((2, share, units), lambda i, h: (0, 1 - h[0], 0)),
            ],
            out_specs=pl.BlockSpec((tile, units), lambda i, h: (i, 0)),
        ),
        compiler_params=pltpu.CompilerParams(vmem_limit_bytes=32 << 20),
        cost_estimate=pl.CostEstimate(
            flops=8 * rows * share * units,
            bytes_accessed=4 * rows * share + 8 * share * units,
            transcendentals=rows * units,
        ),
        name="up_project",
    )(half, mine, other, weights, weights)


def down_project(half, mine, other, weights, w_other):
    rows, units = mine.shape
    share = w_other.shape[0]
    tile = tile_of(rows)
    row_spec = pl.BlockSpec((tile, units), lambda i, h: (i, 0))
    return pl.pallas_call(
        down_kernel,
        out_shape=jax.ShapeDtypeStruct((rows, share), BF16),
        grid_spec=pltpu.PrefetchScalarGridSpec(
            num_scalar_prefetch=1,
            grid=(rows // tile,),
            in_specs=[
                row_spec,
                row_spec,
                pl.BlockSpec((1, share, units), lambda i, h: (2, h[0], 0)),
                pl.BlockSpec((share, units), lambda i, h: (0, 0)),
            ],
            out_specs=pl.BlockSpec((tile, share), lambda i, h: (i, 0)),
        ),
        compiler_params=pltpu.CompilerParams(vmem_limit_bytes=32 << 20),
        cost_estimate=pl.CostEstimate(
            flops=4 * rows * share * units,
            bytes_accessed=4 * rows * units + 4 * share * units + 2 * rows * share,
            transcendentals=0,
        ),
        name="down_project",
    )(half, mine, other, weights, w_other)


def split_gates(gates):
    high = gates.astype(BF16)
    return high, (gates - high.astype(F32)).astype(BF16)


def in_order(blocks):
    block, back13, back2, back4, front4, front2, front13 = blocks
    return [
        block[...],
        back13[0],
        back2[...],
        back13[1],
        back4[...],
        front4[...],
        front13[1],
        front2[...],
        front13[0],
    ]


def pack_kernel(half, tokens, gates, ids, replica, out):
    share = tokens.shape[2]
    top, lanes = replica.shape[0], out.shape[1] - share
    out[:, :share] = tokens[0]
    row = lax.broadcasted_iota(jnp.int32, (top, lanes), 0)
    lane = lax.broadcasted_iota(jnp.int32, (top, lanes), 1)
    numbers = [ids[0], ids[1], replica[...] // 256, replica[...] % 256]
    numbers += [*split_gates(gates[0]), *split_gates(gates[1])]
    total = 0
    for index, part in enumerate(numbers):
        spot = (lane == row + index * top).astype(F32).astype(BF16)
        total += matmul_tn(part.astype(F32).astype(BF16), spot)
    out[:, share:] = total.astype(BF16)


def pack_rows(half, tokens, gate_weights, expert_ids, replica):
    count, share = tokens.shape[1], tokens.shape[2] // 2
    top = replica.shape[1]
    whole = pl.BlockSpec((2, top, count), lambda i, h: (0, 0, 0))
    return pl.pallas_call(
        pack_kernel,
        out_shape=jax.ShapeDtypeStruct((count, share + 128), BF16),
        grid_spec=pltpu.PrefetchScalarGridSpec(
            num_scalar_prefetch=1,
            grid=(1,),
            in_specs=[
                pl.BlockSpec((1, count, share), lambda i, h: (1, 0, h[0])),
                whole,
                whole,
                pl.BlockSpec((top, count), lambda i, h: (0, 0)),
            ],
            out_specs=pl.BlockSpec((count, share + 128), lambda i, h: (0, 0)),
        ),
        name="pack_rows",
    )(
        half,
        tokens,
        jnp.transpose(gate_weights, (0, 2, 1)),
        jnp.transpose(expert_ids, (0, 2, 1)),
        replica.T,
    )


def pick_kernel(first, places, *refs, rows, group):
    blocks, (out, column, ready, done) = refs[:-4], refs[-4:]
    share = column.shape[1]
    start = 0
    for block in in_order(blocks):
        column[start : start + block.shape[0], :] = block[:, :share]
        start += block.shape[0]
    tokens = places.shape[1]
    slots = (lax.broadcasted_iota(jnp.int32, (rows, tokens), 0) + first[0]).astype(F32)
    copies = []
    for index, expert in enumerate(range(0, PLANE, group)):
        hot = [
            jnp.where(places[member : member + 1, :] == slots, 1.0, 0.0).astype(BF16)
            for member in range(expert, expert + group)
        ]
        part = pl.ds(expert * rows, group * rows)
        ready[part, :] = matmul(jnp.concatenate(hot, axis=0), column[...]).astype(BF16)
        copies.append(pltpu.make_async_copy(ready.at[part], out.at[part], done.at[index]))
        copies[-1].start()
    for copy in copies:
        copy.wait()


def pick_rows(places, blocks, first, rows, share):
    tokens = places.shape[1]
    group = 2
    return pl.pallas_call(
        functools.partial(pick_kernel, rows=rows, group=group),
        out_shape=jax.ShapeDtypeStruct((PLANE * rows, share), BF16),
        in_specs=[IN_SMEM, IN_VMEM] + [IN_VMEM] * len(blocks),
        out_specs=pl.BlockSpec(memory_space=pl.ANY),
        scratch_shapes=[
            pltpu.VMEM((tokens, share), BF16),
            pltpu.VMEM((PLANE * rows, share), BF16),
            pltpu.SemaphoreType.DMA((PLANE // group,)),
        ],
        compiler_params=pltpu.CompilerParams(vmem_limit_bytes=32 << 20),
        cost_estimate=pl.CostEstimate(
            flops=2 * PLANE * rows * tokens * share,
            bytes_accessed=2 * PLANE * rows * share + 2 * tokens * share,
            transcendentals=0,
        ),
        name="pick_rows",
    )(first, places, *blocks)


def combine_kernel(
    first, returned, places, gates, near, down, up, half_down, half_up, total, *, rows, group
):
    tokens = places.shape[1]
    count = tokens // DEPTH
    slots = (lax.broadcasted_iota(jnp.int32, (rows, tokens), 0) + first[0]).astype(F32)
    for expert in range(0, PLANE, group):
        high, low = [], []
        for member in range(expert, expert + group):
            here = slice(member, member + 1)
            gate = jnp.where(places[here, :] == slots, gates[here, :], 0.0)
            rounded = gate.astype(BF16)
            high.append(rounded)
            low.append((gate - rounded.astype(F32)).astype(BF16))
        block = returned[expert * rows : (expert + group) * rows, :]
        part = matmul_tn(jnp.concatenate(high, axis=0), block)
        part += matmul_tn(jnp.concatenate(low, axis=0), block)
        if expert == 0:
            total[...] = part
        else:
            total[...] += part

    def sums(back, lo=0, hi=count):
        return total[back * count + lo : back * count + hi, :]

    for index, back in enumerate((0, 2, 6)):
        near[index] = sums(back)
    for index, back in enumerate((1, 3)):
        down[index] = sums(back).astype(BF16)
        up[index] = sums(DEPTH - back).astype(BF16)
    half_down[...] = sums(4, hi=count // 2).astype(BF16)
    half_up[...] = sums(4, lo=count // 2).astype(BF16)


def combine_rows(returned, places, gates, first, rows):
    tokens, share = places.shape[1], returned.shape[1]
    count = tokens // DEPTH
    return pl.pallas_call(
        functools.partial(combine_kernel, rows=rows, group=8),
        out_shape=[
            jax.ShapeDtypeStruct((3, count, share), F32),
            jax.ShapeDtypeStruct((2, count, share), BF16),
            jax.ShapeDtypeStruct((2, count, share), BF16),
            jax.ShapeDtypeStruct((count // 2, share), BF16),
            jax.ShapeDtypeStruct((count // 2, share), BF16),
        ],
        in_specs=[IN_SMEM, IN_VMEM, IN_VMEM, IN_VMEM],
        out_specs=[IN_VMEM] * 5,
        scratch_shapes=[pltpu.VMEM((tokens, share), F32)],
        compiler_params=pltpu.CompilerParams(vmem_limit_bytes=32 << 20),
        cost_estimate=pl.CostEstimate(
            flops=4 * PLANE * rows * tokens * share,
            bytes_accessed=2 * PLANE * rows * share + 4 * tokens * share,
            transcendentals=0,
        ),
        name="combine_rows",
    )(first, returned, places, gates)


def place_kernel(first_expert, plan_row, plan_column, *refs, source_tokens):
    blocks, places, gates = refs[:-2], refs[-2], refs[-1]
    packed = jnp.concatenate(in_order(blocks), axis=0)
    tokens, lanes = packed.shape
    top = lanes // 16
    slots = plan_row.shape[1]
    row = lax.broadcasted_iota(jnp.int32, (lanes // 2, lanes), 0)
    lane = lax.broadcasted_iota(jnp.int32, (lanes // 2, lanes), 1)
    numbers = matmul_nt((row == lane).astype(F32).astype(BF16), packed)

    def number(which, choice):
        return numbers[which * top + choice : which * top + choice + 1, :]

    expert = (lax.broadcasted_iota(jnp.int32, (PLANE, tokens), 0) + first_expert[0]).astype(F32)
    none = jnp.zeros((PLANE, tokens), F32)
    chosen0, chosen1, gates0, gates1, replicas = none, none, none, none, none
    for choice in range(top):
        picked = number(0, choice) == expert
        chosen0 = jnp.where(picked, 1.0, chosen0)
        gates0 = jnp.where(picked, number(4, choice) + number(5, choice), gates0)
        picked = number(1, choice) == expert
        chosen1 = jnp.where(picked, 1.0, chosen1)
        gates1 = jnp.where(picked, number(6, choice) + number(7, choice), gates1)
        replicas = jnp.where(picked, number(2, choice) * 256 + number(3, choice), replicas)
    gates[0] = gates0
    gates[1] = gates1

    holder = lax.broadcasted_iota(jnp.int32, (PLANE, slots), 0) + first_expert[0]
    plan_hot = jnp.where(plan_row[...] == holder, 1.0, 0.0)
    options = 1 + jnp.sum(plan_hot, axis=1, keepdims=True)
    pick = replicas - jnp.floor((replicas + 0.5) / options) * options
    pick = jnp.where(chosen1 > 0, pick, -1.0)
    plan_mat = plan_hot.astype(BF16)
    spare_pick = matmul_tn(plan_mat, pick.astype(BF16))
    slot_row = lax.broadcasted_iota(jnp.int32, (slots, slots), 0)
    slot_lane = lax.broadcasted_iota(jnp.int32, (slots, slots), 1)
    same_before = (plan_row[...] == plan_column[...]) & (slot_lane < slot_row)
    spare_rank = jnp.sum(jnp.where(same_before, 1.0, 0.0), axis=1, keepdims=True)
    in_spare = jnp.where(spare_pick == spare_rank + 1, 1.0, 0.0)
    members = jnp.concatenate([chosen0, jnp.where(pick == 0, 1.0, 0.0), in_spare], axis=0)

    row = lax.broadcasted_iota(jnp.int32, (tokens, tokens), 0)
    lane = lax.broadcasted_iota(jnp.int32, (tokens, tokens), 1)
    before = row < lane
    one_source = row // source_tokens == lane // source_tokens
    ranks = matmul(
        members.astype(BF16), jnp.where(before & one_source, 1.0, 0.0).astype(BF16)
    )
    number_row = lax.broadcasted_iota(jnp.int32, members.shape, 0)
    limit = jnp.where(number_row < PLANE, CAP1, CAP2).astype(F32)
    kept = jnp.where(ranks < limit, members, 0.0)
    kept1 = kept[PLANE : 2 * PLANE] + matmul(plan_mat, kept[2 * PLANE :].astype(BF16))
    kept = jnp.concatenate([kept[:PLANE], kept1], axis=0)
    place = matmul(kept.astype(BF16), jnp.where(before, 1.0, 0.0).astype(BF16))
    place = jnp.where(kept > 0, place, -1.0)
    places[0] = place[:PLANE]
    places[1] = place[PLANE:]


def place_choices(blocks, spare_plan, first_expert, share):
    tokens = DEPTH * blocks[0].shape[0]
    slots = spare_plan.shape[0]
    lanes = blocks[0].shape[1] - share

    def choice_spec(block):
        lead = (0,) * (block.ndim - 1)
        return pl.BlockSpec((*block.shape[:-1], lanes), lambda i, f: (*lead, share // lanes))

    shape = (2, PLANE, tokens)
    table_spec = pl.BlockSpec(shape, lambda i, f: (0, 0, 0))
    return pl.pallas_call(
        functools.partial(place_kernel, source_tokens=tokens // DEPTH),
        out_shape=[jax.ShapeDtypeStruct(shape, F32)] * 2,
        grid_spec=pltpu.PrefetchScalarGridSpec(
            num_scalar_prefetch=1,
            grid=(1,),
            in_specs=[
                pl.BlockSpec((1, slots), lambda i, f: (0, 0)),
                pl.BlockSpec((slots, 1), lambda i, f: (0, 0)),
            ]
            + [choice_spec(block) for block in blocks],
            out_specs=[table_spec, table_spec],
        ),
        compiler_params=pltpu.CompilerParams(vmem_limit_bytes=32 << 20),
        name="place_choices",
    )(first_expert.reshape(1), spare_plan[None, :], spare_plan[:, None], *blocks)


def gather_column(block):
    middle = block.shape[0] // 2
    back2, front2 = shift(block, 2), shift(block, -2)
    back4 = shift(back2[:middle], 2)
    front4 = shift(front2[middle:], -2)
    back13 = shift(jnp.stack([block, back2]), 1)
    front13 = shift(jnp.stack([block, front2]), -1)
    return [block, back13, back2, back4, front4, front2, front13]


def scatter_far(down, up, half_down, half_up):
    return shift(down, -1), shift(up, 1), shift(half_down, -2), shift(half_up, 2)


def scatter_near(blocks):
    to2, to6 = [], []
    for near, (down, up, half_down, half_up) in blocks:
        zeros = jnp.zeros_like(half_down)
        add2 = near[1] + down[1] + jnp.concatenate([half_down, zeros], axis=0)
        add6 = near[2] + up[1] + jnp.concatenate([zeros, half_up], axis=0)
        to2.append(add2.astype(BF16))
        to6.append(add6.astype(BF16))
    return shift(jnp.stack(to2), -2), shift(jnp.stack(to6), 2)


def total_column(blocks, two, six):
    return [
        near[0] + down[0] + up[0] + two[index] + six[index]
        for index, (near, (down, up, _, _)) in enumerate(blocks)
    ]


def exchange_plane(rows):
    wide = rows.reshape(PLANE, -1, rows.shape[1])
    return lax.all_to_all(
        wide, PLANE_AXES, split_axis=0, concat_axis=0, tiled=True
    ).reshape(rows.shape)


def local(tokens, gate_weights, expert_ids, replica, spare_plan, w_experts):
    half = lax.axis_index("dp").astype(jnp.int32)
    count, share = tokens.shape[1], tokens.shape[2] // 2
    half_arg = half.reshape(1)
    weights = jnp.transpose(w_experts[0], (1, 0, 2))

    first_expert = lax.axis_index("z").astype(jnp.int32) * PLANE
    blocks1 = gather_column(pack_rows(half_arg, tokens, gate_weights, expert_ids, replica))
    mine0 = lax.dynamic_slice_in_dim(tokens[0], half * share, share, axis=1)
    blocks1, mine0 = lax.optimization_barrier((blocks1, mine0))
    places, gates = place_choices(blocks1, spare_plan, first_expert, share)

    def pick(block, blocks, rows, first):
        first = jnp.asarray(first, jnp.int32).reshape(1)
        return pick_rows(places[block], blocks, first, rows, share)

    def experts(received, down_other):
        partner = lax.ppermute(received, "dp", SWAP)
        hidden = up_project(half_arg, received, partner, weights)
        partner_hidden = lax.ppermute(hidden, "dp", SWAP)
        return down_project(half_arg, hidden, partner_hidden, weights, down_other)

    def combine(block, returned, rows, first):
        first = jnp.asarray(first, jnp.int32).reshape(1)
        near, *parts = combine_rows(returned, places[block], gates[block], first, rows)
        return near, scatter_far(*parts)

    def run(batch, rounds):
        picked1 = pick(1, blocks1, batch, 0)
        blocks0 = gather_column(mine0)
        received1 = exchange_plane(picked1)
        picked0 = pick(0, blocks0, BATCH0, 0)
        down_rows = lax.dynamic_slice(
            weights, (2, (1 - half) * share, 0), (1, share, weights.shape[2])
        )
        down_other = lax.ppermute(down_rows[0], "dp", SWAP)
        received1, picked0, down_other = lax.optimization_barrier(
            (received1, picked0, down_other)
        )
        received0 = exchange_plane(picked0)
        outputs1 = experts(received1, down_other)
        outputs1, received0 = lax.optimization_barrier((outputs1, received0))
        returned1 = exchange_plane(outputs1)
        outputs0 = experts(received0, down_other)
        returned1, outputs0 = lax.optimization_barrier((returned1, outputs0))
        returned0 = exchange_plane(outputs0)
        second = combine(1, returned1, batch, 0)
        returned0, second = lax.optimization_barrier((returned0, second))
        first = combine(0, returned0, BATCH0, 0)
        total0, total1 = total_column([first, second], *scatter_near([first, second]))

        def another_round(step, total):
            outgoing = pick(1, blocks1, batch, step * batch)
            returned = exchange_plane(experts(exchange_plane(outgoing), down_other))
            sums = [combine(1, returned, batch, step * batch)]
            return total + total_column(sums, *scatter_near(sums))[0]

        if rounds is not None:
            total1 = lax.fori_loop(1, rounds, another_round, total1)
        return jnp.stack([total0, total1]).astype(BF16)

    same = spare_plan[:, None] == spare_plan[None, :]
    most = jnp.max(jnp.sum(same.astype(jnp.int32), axis=1))
    most_rows = DEPTH * jnp.minimum(CAP2 * (1 + most), count)
    largest = BATCH1[-1]
    branches = [functools.partial(run, batch, None) for batch in BATCH1]
    branches.append(lambda: run(largest, (most_rows + largest - 1) // largest))
    return lax.switch(sum((most_rows > batch).astype(jnp.int32) for batch in BATCH1), branches)


def solution(mesh):
    grid = Mesh(np.asarray(mesh.devices).reshape(DEPTH, ROW, ROW, 2), ("z", "x", "y", "dp"))
    in_specs = (
        P(None, ALL_AXES, None),
        P(None, ALL_AXES, None),
        P(None, ALL_AXES, None),
        P(ALL_AXES, None),
        P(),
        P(ALL_AXES, None, None, "dp"),
    )
    out_specs = P(None, ALL_AXES, "dp")
    return jax.shard_map(local, mesh=grid, in_specs=in_specs, out_specs=out_specs, check_vma=False)
```

```python
import functools

import jax
import jax.numpy as jnp
import numpy as np
from jax import lax
from jax.experimental import pallas as pl
from jax.experimental.pallas import tpu as pltpu
from jax.sharding import Mesh
from jax.sharding import PartitionSpec as P

CAP1 = 6
CAP2 = 2
DEPTH = 8
ROW = 4
PLANE = ROW * ROW
BATCH0 = DEPTH * CAP1
BATCH1 = 96
TILE = 384
PLANE_AXES = ("x", "y")
ALL_AXES = ("z", "x", "y")
SWAP = [(0, 1), (1, 0)]
IN_VMEM = pl.BlockSpec(memory_space=pltpu.VMEM)
IN_SMEM = pl.BlockSpec(memory_space=pltpu.SMEM)
BF16 = jnp.bfloat16
F32 = jnp.float32


def matmul(left, right):
    return jnp.dot(left, right, preferred_element_type=F32)


def matmul_nt(left, right):
    return lax.dot_general(left, right, (((1,), (1,)), ((), ())), preferred_element_type=F32)


def matmul_tn(left, right):
    return lax.dot_general(left, right, (((0,), (0,)), ((), ())), preferred_element_type=F32)


def shift(block, step):
    return lax.ppermute(block, "z", [(i, (i + step) % DEPTH) for i in range(DEPTH)])


def up_kernel(half, mine, other, w_mine, w_other, out):
    def project(which):
        return matmul(mine[...], w_mine[which]) + matmul(other[...], w_other[which])

    gate = project(0)
    out[...] = (gate / (1 + jnp.exp(-gate)) * project(1)).astype(BF16)


def down_kernel(half, mine, other, w_mine, w_other, out):
    out[...] = (matmul_nt(mine[...], w_mine[0]) + matmul_nt(other[...], w_other[...])).astype(BF16)


def up_project(half, mine, other, weights):
    rows, share = mine.shape
    units = weights.shape[2]
    row_spec = pl.BlockSpec((TILE, share), lambda i, h: (i, 0))
    return pl.pallas_call(
        up_kernel,
        out_shape=jax.ShapeDtypeStruct((rows, units), BF16),
        grid_spec=pltpu.PrefetchScalarGridSpec(
            num_scalar_prefetch=1,
            grid=(rows // TILE,),
            in_specs=[
                row_spec,
                row_spec,
                pl.BlockSpec((2, share, units), lambda i, h: (0, h[0], 0)),
                pl.BlockSpec((2, share, units), lambda i, h: (0, 1 - h[0], 0)),
            ],
            out_specs=pl.BlockSpec((TILE, units), lambda i, h: (i, 0)),
        ),
        compiler_params=pltpu.CompilerParams(vmem_limit_bytes=32 << 20),
        cost_estimate=pl.CostEstimate(
            flops=8 * rows * share * units,
            bytes_accessed=4 * rows * share + 8 * share * units,
            transcendentals=rows * units,
        ),
        name="up_project",
    )(half, mine, other, weights, weights)


def down_project(half, mine, other, weights, w_other):
    rows, units = mine.shape
    share = w_other.shape[0]
    row_spec = pl.BlockSpec((TILE, units), lambda i, h: (i, 0))
    return pl.pallas_call(
        down_kernel,
        out_shape=jax.ShapeDtypeStruct((rows, share), BF16),
        grid_spec=pltpu.PrefetchScalarGridSpec(
            num_scalar_prefetch=1,
            grid=(rows // TILE,),
            in_specs=[
                row_spec,
                row_spec,
                pl.BlockSpec((1, share, units), lambda i, h: (2, h[0], 0)),
                pl.BlockSpec((share, units), lambda i, h: (0, 0)),
            ],
            out_specs=pl.BlockSpec((TILE, share), lambda i, h: (i, 0)),
        ),
        compiler_params=pltpu.CompilerParams(vmem_limit_bytes=32 << 20),
        cost_estimate=pl.CostEstimate(
            flops=4 * rows * share * units,
            bytes_accessed=4 * rows * units + 4 * share * units + 2 * rows * share,
            transcendentals=0,
        ),
        name="down_project",
    )(half, mine, other, weights, w_other)


def split_gates(gates):
    high = gates.astype(BF16)
    return high, (gates - high.astype(F32)).astype(BF16)


def in_order(blocks):
    block, back13, back2, back4, front4, front2, front13 = blocks
    return [
        block[...],
        back13[0],
        back2[...],
        back13[1],
        back4[...],
        front4[...],
        front13[1],
        front2[...],
        front13[0],
    ]


def pack_kernel(half, tokens, gates, ids, replica, out):
    share = tokens.shape[2]
    top, lanes = replica.shape[0], out.shape[1] - share
    out[:, :share] = tokens[0]
    row = lax.broadcasted_iota(jnp.int32, (top, lanes), 0)
    lane = lax.broadcasted_iota(jnp.int32, (top, lanes), 1)
    numbers = [ids[0], ids[1], replica[...] // 256, replica[...] % 256]
    numbers += [*split_gates(gates[0]), *split_gates(gates[1])]
    total = 0
    for index, part in enumerate(numbers):
        spot = (lane == row + index * top).astype(F32).astype(BF16)
        total += matmul_tn(part.astype(F32).astype(BF16), spot)
    out[:, share:] = total.astype(BF16)


def pack_rows(half, tokens, gate_weights, expert_ids, replica):
    count, share = tokens.shape[1], tokens.shape[2] // 2
    top = replica.shape[1]
    whole = pl.BlockSpec((2, top, count), lambda i, h: (0, 0, 0))
    return pl.pallas_call(
        pack_kernel,
        out_shape=jax.ShapeDtypeStruct((count, share + 128), BF16),
        grid_spec=pltpu.PrefetchScalarGridSpec(
            num_scalar_prefetch=1,
            grid=(1,),
            in_specs=[
                pl.BlockSpec((1, count, share), lambda i, h: (1, 0, h[0])),
                whole,
                whole,
                pl.BlockSpec((top, count), lambda i, h: (0, 0)),
            ],
            out_specs=pl.BlockSpec((count, share + 128), lambda i, h: (0, 0)),
        ),
        name="pack_rows",
    )(
        half,
        tokens,
        jnp.transpose(gate_weights, (0, 2, 1)),
        jnp.transpose(expert_ids, (0, 2, 1)),
        replica.T,
    )


def pick_kernel(first, places, *refs, rows, group):
    blocks, out, column = refs[:-2], refs[-2], refs[-1]
    share = column.shape[1]
    start = 0
    for block in in_order(blocks):
        column[start : start + block.shape[0], :] = block[:, :share]
        start += block.shape[0]
    tokens = places.shape[1]
    slots = (lax.broadcasted_iota(jnp.int32, (rows, tokens), 0) + first[0]).astype(F32)
    for expert in range(0, PLANE, group):
        hot = [
            jnp.where(places[member : member + 1, :] == slots, 1.0, 0.0).astype(BF16)
            for member in range(expert, expert + group)
        ]
        picked = matmul(jnp.concatenate(hot, axis=0), column[...]).astype(BF16)
        out[expert * rows : (expert + group) * rows, :] = picked


def pick_rows(places, blocks, first, rows, share):
    tokens = places.shape[1]
    return pl.pallas_call(
        functools.partial(pick_kernel, rows=rows, group=4),
        out_shape=jax.ShapeDtypeStruct((PLANE * rows, share), BF16),
        in_specs=[IN_SMEM, IN_VMEM] + [IN_VMEM] * len(blocks),
        out_specs=IN_VMEM,
        scratch_shapes=[pltpu.VMEM((tokens, share), BF16)],
        compiler_params=pltpu.CompilerParams(vmem_limit_bytes=32 << 20),
        cost_estimate=pl.CostEstimate(
            flops=2 * PLANE * rows * tokens * share,
            bytes_accessed=2 * PLANE * rows * share + 2 * tokens * share,
            transcendentals=0,
        ),
        name="pick_rows",
    )(first, places, *blocks)


def combine_kernel(
    first, returned, places, gates, near, down, up, half_down, half_up, total, *, rows, group
):
    tokens = places.shape[1]
    count = tokens // DEPTH
    slots = (lax.broadcasted_iota(jnp.int32, (rows, tokens), 0) + first[0]).astype(F32)
    for expert in range(0, PLANE, group):
        high, low = [], []
        for member in range(expert, expert + group):
            here = slice(member, member + 1)
            gate = jnp.where(places[here, :] == slots, gates[here, :], 0.0)
            rounded = gate.astype(BF16)
            high.append(rounded)
            low.append((gate - rounded.astype(F32)).astype(BF16))
        block = returned[expert * rows : (expert + group) * rows, :]
        part = matmul_tn(jnp.concatenate(high, axis=0), block)
        part += matmul_tn(jnp.concatenate(low, axis=0), block)
        if expert == 0:
            total[...] = part
        else:
            total[...] += part

    def sums(back, lo=0, hi=count):
        return total[back * count + lo : back * count + hi, :]

    for index, back in enumerate((0, 2, 6)):
        near[index] = sums(back)
    for index, back in enumerate((1, 3)):
        down[index] = sums(back).astype(BF16)
        up[index] = sums(DEPTH - back).astype(BF16)
    half_down[...] = sums(4, hi=count // 2).astype(BF16)
    half_up[...] = sums(4, lo=count // 2).astype(BF16)


def combine_rows(returned, places, gates, first, rows):
    tokens, share = places.shape[1], returned.shape[1]
    count = tokens // DEPTH
    return pl.pallas_call(
        functools.partial(combine_kernel, rows=rows, group=8),
        out_shape=[
            jax.ShapeDtypeStruct((3, count, share), F32),
            jax.ShapeDtypeStruct((2, count, share), BF16),
            jax.ShapeDtypeStruct((2, count, share), BF16),
            jax.ShapeDtypeStruct((count // 2, share), BF16),
            jax.ShapeDtypeStruct((count // 2, share), BF16),
        ],
        in_specs=[IN_SMEM, IN_VMEM, IN_VMEM, IN_VMEM],
        out_specs=[IN_VMEM] * 5,
        scratch_shapes=[pltpu.VMEM((tokens, share), F32)],
        compiler_params=pltpu.CompilerParams(vmem_limit_bytes=32 << 20),
        cost_estimate=pl.CostEstimate(
            flops=4 * PLANE * rows * tokens * share,
            bytes_accessed=2 * PLANE * rows * share + 4 * tokens * share,
            transcendentals=0,
        ),
        name="combine_rows",
    )(first, returned, places, gates)


def place_kernel(first_expert, plan_row, *refs, source_tokens):
    blocks, places, gates = refs[:-2], refs[-2], refs[-1]
    packed = jnp.concatenate(in_order(blocks), axis=0)
    tokens, lanes = packed.shape
    top = lanes // 16
    slots = plan_row.shape[1]
    row = lax.broadcasted_iota(jnp.int32, (lanes // 2, lanes), 0)
    lane = lax.broadcasted_iota(jnp.int32, (lanes // 2, lanes), 1)
    numbers = matmul_nt((row == lane).astype(F32).astype(BF16), packed)

    def number(which, choice):
        return numbers[which * top + choice : which * top + choice + 1, :]

    expert = (lax.broadcasted_iota(jnp.int32, (PLANE, tokens), 0) + first_expert[0]).astype(F32)
    none = jnp.zeros((PLANE, tokens), F32)
    chosen0, chosen1, gates0, gates1, replicas = none, none, none, none, none
    for choice in range(top):
        picked = number(0, choice) == expert
        chosen0 = jnp.where(picked, 1.0, chosen0)
        gates0 = jnp.where(picked, number(4, choice) + number(5, choice), gates0)
        picked = number(1, choice) == expert
        chosen1 = jnp.where(picked, 1.0, chosen1)
        gates1 = jnp.where(picked, number(6, choice) + number(7, choice), gates1)
        replicas = jnp.where(picked, number(2, choice) * 256 + number(3, choice), replicas)
    gates[0] = gates0
    gates[1] = gates1

    holder = lax.broadcasted_iota(jnp.int32, (PLANE, slots), 0) + first_expert[0]
    plan_hot = jnp.where(plan_row[...] == holder, 1.0, 0.0)
    options = 1 + jnp.sum(plan_hot, axis=1, keepdims=True)
    pick = replicas - jnp.floor((replicas + 0.5) / options) * options
    pick = jnp.where(chosen1 > 0, pick, -1.0)
    plan_mat = plan_hot.astype(BF16)
    spare_pick = matmul_tn(plan_mat, pick.astype(BF16))
    slot_row = lax.broadcasted_iota(jnp.int32, (slots, slots), 0)
    slot_lane = lax.broadcasted_iota(jnp.int32, (slots, slots), 1)
    plan_column = jnp.sum(
        jnp.where(slot_row == slot_lane, plan_row[...], 0), axis=1, keepdims=True
    )
    same_before = (plan_row[...] == plan_column) & (slot_lane < slot_row)
    spare_rank = jnp.sum(jnp.where(same_before, 1.0, 0.0), axis=1, keepdims=True)
    in_spare = jnp.where(spare_pick == spare_rank + 1, 1.0, 0.0)
    members = jnp.concatenate([chosen0, jnp.where(pick == 0, 1.0, 0.0), in_spare], axis=0)

    row = lax.broadcasted_iota(jnp.int32, (tokens, tokens), 0)
    lane = lax.broadcasted_iota(jnp.int32, (tokens, tokens), 1)
    before = row < lane
    one_source = row // source_tokens == lane // source_tokens
    ranks = matmul(
        members.astype(BF16), jnp.where(before & one_source, 1.0, 0.0).astype(BF16)
    )
    number_row = lax.broadcasted_iota(jnp.int32, members.shape, 0)
    limit = jnp.where(number_row < PLANE, CAP1, CAP2).astype(F32)
    kept = jnp.where(ranks < limit, members, 0.0)
    kept1 = kept[PLANE : 2 * PLANE] + matmul(plan_mat, kept[2 * PLANE :].astype(BF16))
    kept = jnp.concatenate([kept[:PLANE], kept1], axis=0)
    place = matmul(kept.astype(BF16), jnp.where(before, 1.0, 0.0).astype(BF16))
    place = jnp.where(kept > 0, place, -1.0)
    places[0] = place[:PLANE]
    places[1] = place[PLANE:]


def place_choices(blocks, spare_plan, first_expert, share):
    tokens = DEPTH * blocks[0].shape[0]
    slots = spare_plan.shape[0]
    lanes = blocks[0].shape[1] - share

    def choice_spec(block):
        lead = (0,) * (block.ndim - 1)
        return pl.BlockSpec((*block.shape[:-1], lanes), lambda i, f: (*lead, share // lanes))

    shape = (2, PLANE, tokens)
    table_spec = pl.BlockSpec(shape, lambda i, f: (0, 0, 0))
    return pl.pallas_call(
        functools.partial(place_kernel, source_tokens=tokens // DEPTH),
        out_shape=[jax.ShapeDtypeStruct(shape, F32)] * 2,
        grid_spec=pltpu.PrefetchScalarGridSpec(
            num_scalar_prefetch=1,
            grid=(1,),
            in_specs=[pl.BlockSpec((1, slots), lambda i, f: (0, 0))]
            + [choice_spec(block) for block in blocks],
            out_specs=[table_spec, table_spec],
        ),
        compiler_params=pltpu.CompilerParams(vmem_limit_bytes=32 << 20),
        name="place_choices",
    )(first_expert.reshape(1), spare_plan[None, :], *blocks)


def gather_column(block):
    middle = block.shape[0] // 2
    back2, front2 = shift(block, 2), shift(block, -2)
    back4 = shift(back2[:middle], 2)
    front4 = shift(front2[middle:], -2)
    back13 = shift(jnp.stack([block, back2]), 1)
    front13 = shift(jnp.stack([block, front2]), -1)
    return [block, back13, back2, back4, front4, front2, front13]


def scatter_far(down, up, half_down, half_up):
    return shift(down, -1), shift(up, 1), shift(half_down, -2), shift(half_up, 2)


def relay(sums):
    near, (down, up, half_down, half_up) = sums
    zeros = jnp.zeros_like(half_down)
    to2 = near[1] + down[1] + jnp.concatenate([half_down, zeros], axis=0)
    to6 = near[2] + up[1] + jnp.concatenate([zeros, half_up], axis=0)
    return to2.astype(BF16), to6.astype(BF16)


def scatter_near(to2, to6):
    return shift(to2, -2), shift(to6, 2)


def total_column(sums, received):
    near, (down, up, _, _) = sums
    two, six = received
    return near[0] + down[0] + up[0] + two + six


def exchange_plane(rows):
    wide = rows.reshape(PLANE, -1, rows.shape[1])
    return lax.all_to_all(
        wide, PLANE_AXES, split_axis=0, concat_axis=0, tiled=True
    ).reshape(rows.shape)


def local(tokens, gate_weights, expert_ids, replica, spare_plan, w_experts):
    half = lax.axis_index("dp").astype(jnp.int32)
    count, share = tokens.shape[1], tokens.shape[2] // 2
    half_arg = half.reshape(1)
    weights = jnp.transpose(w_experts[0], (1, 0, 2))

    first_expert = lax.axis_index("z").astype(jnp.int32) * PLANE
    blocks1 = gather_column(pack_rows(half_arg, tokens, gate_weights, expert_ids, replica))
    later_half, blocks1[2] = lax.optimization_barrier((half, blocks1[2]))
    mine0 = lax.dynamic_slice_in_dim(tokens[0], half * share, share, axis=1)
    blocks1, mine0 = lax.optimization_barrier((blocks1, mine0))
    down_rows = lax.dynamic_slice(
        weights, (2, (1 - later_half) * share, 0), (1, share, weights.shape[2])
    )
    down_other = lax.ppermute(down_rows[0], "dp", SWAP)
    places, gates = place_choices(blocks1, spare_plan, first_expert, share)

    def pick(block, blocks, rows, first):
        first = jnp.asarray(first, jnp.int32).reshape(1)
        return pick_rows(places[block], blocks, first, rows, share)

    def experts(received, down_other):
        partner = lax.ppermute(received, "dp", SWAP)
        hidden = up_project(half_arg, received, partner, weights)
        partner_hidden = lax.ppermute(hidden, "dp", SWAP)
        return down_project(half_arg, hidden, partner_hidden, weights, down_other)

    def combine(block, returned, rows, first):
        first = jnp.asarray(first, jnp.int32).reshape(1)
        near, *parts = combine_rows(returned, places[block], gates[block], first, rows)
        return near, scatter_far(*parts)

    picked1 = pick(1, blocks1, BATCH1, 0)
    blocks0 = gather_column(mine0)
    received1 = exchange_plane(picked1)
    picked0 = pick(0, blocks0, BATCH0, 0)
    received1, picked0, down_other = lax.optimization_barrier((received1, picked0, down_other))
    received0 = exchange_plane(picked0)
    outputs1 = experts(received1, down_other)
    outputs1, received0 = lax.optimization_barrier((outputs1, received0))
    returned1 = exchange_plane(outputs1)
    outputs0 = experts(received0, down_other)
    returned1, outputs0 = lax.optimization_barrier((returned1, outputs0))
    returned0 = exchange_plane(outputs0)
    second = combine(1, returned1, BATCH1, 0)
    relayed1 = relay(second)
    returned0, second, relayed1 = lax.optimization_barrier((returned0, second, relayed1))
    near1 = scatter_near(*relayed1)
    first = combine(0, returned0, BATCH0, 0)
    near0 = scatter_near(*relay(first))

    def another_round(step, total):
        outgoing = pick(1, blocks1, BATCH1, step * BATCH1)
        returned = exchange_plane(experts(exchange_plane(outgoing), down_other))
        sums = combine(1, returned, BATCH1, step * BATCH1)
        return total + total_column(sums, scatter_near(*relay(sums)))

    def usual():
        return jnp.stack([total_column(first, near0), total_column(second, near1)]).astype(BF16)

    def with_more_rounds():
        total1 = lax.fori_loop(1, rounds, another_round, total_column(second, near1))
        return jnp.stack([total_column(first, near0), total1]).astype(BF16)

    same = spare_plan[:, None] == spare_plan[None, :]
    most = jnp.max(jnp.sum(same.astype(jnp.int32), axis=1))
    most_rows = DEPTH * jnp.minimum(CAP2 * (1 + most), count)
    rounds = (most_rows + BATCH1 - 1) // BATCH1
    return lax.cond(rounds > 1, with_more_rounds, usual)


def solution(mesh):
    grid = Mesh(np.asarray(mesh.devices).reshape(DEPTH, ROW, ROW, 2), ("z", "x", "y", "dp"))
    in_specs = (
        P(None, ALL_AXES, None),
        P(None, ALL_AXES, None),
        P(None, ALL_AXES, None),
        P(ALL_AXES, None),
        P(),
        P(ALL_AXES, None, None, "dp"),
    )
    out_specs = P(None, ALL_AXES, "dp")
    return jax.shard_map(local, mesh=grid, in_specs=in_specs, out_specs=out_specs, check_vma=False)
```
